256 devices in a mesh: dp: 16 (over z, core), tensor: 16 (over y, x).
Axes of the slice: x: 4, y: 4, z: 8, core: 2. Of those that a mesh axis runs over, the one named last changes fastest.
Arguments:
- upstream: bfloat16 [4096, 8192], P(('dp', 'tensor')), may hold values from -24 to 24
- out_weight: bfloat16 [8192, 10240], P(None, 'tensor'), may hold values from -0.0625 to 0.0625
- inner: bfloat16 [4096, 10240], P('dp', 'tensor'), may hold values from -6 to 6
- groups_bc: bfloat16 [4096, 8192], P('dp', 'tensor'), may hold values from -1.5 to 1.5
- dt_raw: float32 [160, 4096], P('tensor', 'dp'), may hold values from -3 to 3
- a_log: float32 [160], P('tensor'), may hold values from 0 to 2.77
- skip: float32 [160], P('tensor'), may hold values from 0.5 to 1.5
- dt_bias: float32 [160], P('tensor'), may hold values from -4.5 to -1
- head_counts: int32 [16], replicated, may hold values from 1 to 10, 128 in all
Outputs:
- inner_grad: bfloat16 [4096, 10240], P('dp', 'tensor')
- groups_grad: bfloat16 [4096, 8192], P('dp', 'tensor')
- dt_grad: float32 [160, 4096], P('tensor', 'dp')
- weight_grad: float32 [8192, 10240], P('dp', 'tensor')
- head_grads: float32 [3, 160], P(None, 'tensor')
The draws below stay inside these ranges and needn't reach their ends.
Inputs may be any that keep to these rules, and one draw needn't show every extreme that they name: `head_counts`: heads in use in each tensor group; the other slots of its 10 are padding; they sum to 128.
All inputs are finite; a program needn't handle non-finite values.
Results may differ from the reference program's by a relative error of at most 0.0029.
Values may be sent and summed in bfloat16 or wider, within the bound.
A program may use at most 128 MiB of HBM per device.

```python
import math
import jax
import jax.numpy as jnp
import numpy as np
from jax import lax

D = 8192
P_SIZE = 64
N = 256
HMAX = 10
BLOCK = 128
SEQ = 256
HEADS = 128
HEADS_PAD = 160
TOKENS = 4096
N_DP = 16
N_TENSOR = 16


def raised(array, stream_key, source, target, shards_of, factor):
    owner, partner = [(jnp.arange(array.shape[dim]) // (array.shape[dim] // shards_of)).reshape([-1 if axis == dim else 1 for axis in range(array.ndim)]) for dim in (source, target)]
    chosen = jax.random.permutation(stream_key, shards_of)[partner]
    strong = (owner == chosen) | (owner == (partner + shards_of // 2) % shards_of)
    return jnp.where(strong, factor * array, array)


def block_levels(own_key, dims, cuts, low, largest):
    loudness = 1.0
    for axis_at, shards_of in cuts:
        steps = jax.random.uniform(jax.random.fold_in(jax.random.fold_in(own_key, 6), axis_at), (shards_of,), jnp.float32, low / len(cuts), largest / len(cuts))
        loudness = loudness * jnp.repeat(jnp.exp(steps), dims[axis_at] // shards_of).reshape((-1,) + (1,) * (len(dims) - 1 - axis_at))
    return loudness


def split_up(number_of, total, most, skew):
    portions = [(1 << 20) // math.isqrt(rank ** skew) + 1 for rank in range(2, number_of + 1)]
    surplus, holding = total - most - (number_of - 1), [1] * (number_of - 1)
    while surplus > 0:
        candidates = [i for i in range(number_of - 1) if holding[i] < most]
        whole, budget = sum([portions[i] for i in candidates]), surplus
        for i in candidates:
            extra = min(most - holding[i], max(1, budget * portions[i] // whole), surplus)
            holding[i] = holding[i] + extra
            surplus = surplus - extra
    return np.array([most] + holding)


def ragged_sizes(key, number_of, total, limit, skew):
    if number_of == 2:
        one = jax.random.randint(key, (), max(1, total - limit), min(limit, total - 1) + 1)
        return jnp.stack([one, total - one])
    sizes = jnp.asarray(split_up(number_of, total, limit, skew), jnp.int32)
    couples = (number_of - 1) // 2
    donor, sink = sizes[1:1 + 2 * couples:2], sizes[2:2 + 2 * couples:2]
    margin = jnp.minimum(donor - 1, limit - sink)
    shifted = jax.random.randint(jax.random.fold_in(key, 1), (couples,), 0, 1 << 20) % (margin + 1)
    sizes = sizes.at[1:1 + 2 * couples:2].set(donor - shifted).at[2:2 + 2 * couples:2].set(sink + shifted)
    return sizes[jax.random.permutation(jax.random.fold_in(key, 2), number_of)]


def normal_values(own_key, dims, spread, limit, pieces=(), held_as=jnp.bfloat16):
    values = jax.random.normal(own_key, dims, jnp.float32) * spread
    if len(pieces) > 0:
        values = block_levels(own_key, dims, pieces, -0.22, 0.18) * values
    return jnp.clip(values, min=-limit, max=limit).astype(held_as)


def heavy_noise(rng, extent, scale, bound, shards, heavy, kind=jnp.bfloat16):
    drawn = scale * jax.random.normal(rng, extent, jnp.float32)
    if shards:
        drawn = drawn * block_levels(rng, extent, shards, -0.22, 0.18)
    return jnp.clip(raised(drawn, jax.random.fold_in(rng, 3), *heavy), -bound, bound).astype(kind)


def setup_inputs(seed: int = 0) -> dict:
    key_of = jax.random.split(jax.random.key(seed), 10)
    upstream = heavy_noise(key_of[0], (TOKENS, D), 1.0, 24.0, ((0, 256),), (0, 1, 256, 6.0))
    out_weight = normal_values(key_of[1], (D, HEADS_PAD * P_SIZE), (HEADS * P_SIZE) ** -0.5, 0.0625, ((1, 16),))
    inner = normal_values(key_of[2], (TOKENS, HEADS_PAD * P_SIZE), 1.0, 6.0, ((0, 16), (1, 16)))
    groups_bc = normal_values(key_of[3], (TOKENS, N_TENSOR * 2 * N), (N ** -0.25), 1.5, ((0, 16), (1, 16)))
    dt_raw = normal_values(key_of[4], (HEADS_PAD, TOKENS), 0.5, 3.0, ((0, 16), (1, 16)), jnp.float32)
    a_log = jnp.clip(2.77 * jax.random.uniform(key_of[5], (HEADS_PAD,), jnp.float32) ** block_levels(key_of[5], (HEADS_PAD,), ((0, 16),), -0.2, 0.2), 0.0, 2.77)
    skip = jnp.clip(0.5 + 1.0 * jax.random.uniform(key_of[6], (HEADS_PAD,), jnp.float32) ** block_levels(key_of[6], (HEADS_PAD,), ((0, 16),), -0.2, 0.2), 0.5, 1.5)
    dt_bias = jnp.clip(-4.5 + 3.5 * jax.random.uniform(key_of[7], (HEADS_PAD,), jnp.float32) ** block_levels(key_of[7], (HEADS_PAD,), ((0, 16),), -0.2, 0.2), -4.5, -1.0)
    head_counts = ragged_sizes(key_of[8], N_TENSOR, HEADS, HMAX, 1).astype(jnp.int32)
    return {"upstream": upstream, "out_weight": out_weight, "inner": inner, "groups_bc": groups_bc, "dt_raw": dt_raw, "a_log": a_log, "skip": skip, "dt_bias": dt_bias, "head_counts": head_counts}


def scan_heads(inner, groups_bc, dt_raw, a_log, skip, dt_bias, active):
    length = inner.shape[0]
    head_slots = a_log.shape[0]
    head_width = inner.shape[1] // head_slots
    state_size = groups_bc.shape[1] // 2
    blocks = length // BLOCK
    highest_precision = lax.Precision.HIGHEST
    values = inner.astype(jnp.float32).reshape(blocks, BLOCK, head_slots, head_width)
    projected = groups_bc.astype(jnp.float32).reshape(blocks, BLOCK, 2 * state_size)
    entry_vectors_list = projected[:, :, :state_size]
    readout_matrix = projected[:, :, state_size:]
    step_sizes = jax.nn.softplus(dt_raw + dt_bias[:, None]).reshape(head_slots, blocks, BLOCK)
    rates = step_sizes * jnp.exp(a_log)[:, None, None]
    totals = jnp.cumsum(rates, axis=2)
    scaled_inputs = values * jnp.transpose(step_sizes, (1, 2, 0))[:, :, :, None]
    score_matrix = jnp.einsum('adw,ahw->adh', readout_matrix, entry_vectors_list, precision=highest_precision)
    causal = jnp.arange(BLOCK)[:, None] >= jnp.arange(BLOCK)[None, :]
    decay_gaps = totals[:, :, :, None] - totals[:, :, None, :]
    weight_matrix = jnp.where(causal, jnp.exp(-jnp.where(causal, decay_gaps, 0.0)), 0.0)
    local_portion = jnp.einsum('ocmi,cmi,ciof->cmof', weight_matrix, score_matrix, scaled_inputs, precision=highest_precision)
    to_end = jnp.exp(totals - totals[:, :, -1:])
    block_states = jnp.einsum('hbk,bkn,bkhp->bhnp', to_end, entry_vectors_list, scaled_inputs, precision=highest_precision)
    running = jnp.zeros((head_slots, state_size, head_width), jnp.float32)
    entering = []
    for position in range(blocks):
        entering.append(running)
        running = jnp.exp(-totals[:, position, -1])[:, None, None] * running + block_states[position]
    entering = jnp.stack(entering)
    carried_part = jnp.einsum('bqn,hbq,bhnp->bqhp', readout_matrix, jnp.exp(-totals), entering, precision=highest_precision)
    result = (local_portion + carried_part + skip[None, None, :, None] * values) * active[None, None, :, None]
    return result.reshape(length, head_slots * head_width)

def reference(upstream, out_weight, inner, groups_bc, dt_raw, a_log, skip, dt_bias, head_counts):
    slot_width = HMAX * P_SIZE
    ranks = jnp.arange(N_TENSOR, dtype=jnp.int32)

    def per_rank(tensor_rank):
        weight = lax.dynamic_slice_in_dim(out_weight, tensor_rank * slot_width, slot_width, 1)
        inner_rank = lax.dynamic_slice_in_dim(inner, tensor_rank * slot_width, slot_width, 1)
        pairs_rank = lax.dynamic_slice_in_dim(groups_bc, tensor_rank * (2 * N), 2 * N, 1)
        steps_rank = lax.dynamic_slice_in_dim(dt_raw, tensor_rank * HMAX, HMAX, 0)
        alog_rank = lax.dynamic_slice_in_dim(a_log, tensor_rank * HMAX, HMAX, 0)
        skip_rank = lax.dynamic_slice_in_dim(skip, tensor_rank * HMAX, HMAX, 0)
        bias_rank = lax.dynamic_slice_in_dim(dt_bias, tensor_rank * HMAX, HMAX, 0)
        used_heads = jnp.sum(jnp.where(ranks == tensor_rank, head_counts, 0))
        active = (jnp.arange(HMAX, dtype=jnp.int32) < used_heads).astype(jnp.float32)

        def per_block(running, block_index):
            start = (block_index * SEQ).astype(jnp.int32)
            upstream_block = lax.dynamic_slice_in_dim(upstream, start, SEQ, 0)
            inner_block = lax.dynamic_slice_in_dim(inner_rank, start, SEQ, 0)
            pairs_block = lax.dynamic_slice_in_dim(pairs_rank, start, SEQ, 0)
            steps_block = lax.dynamic_slice_in_dim(steps_rank, start, SEQ, 1)
            flat_grad = jnp.dot(upstream_block, weight, preferred_element_type=jnp.float32)

            def forward(values, pairs, steps, alog, direct, bias):
                return scan_heads(values, pairs, steps, alog, direct, bias, active)
            outputs, pullback = jax.vjp(forward, inner_block, pairs_block, steps_block, alog_rank, skip_rank, bias_rank)
            inner_g, pairs_g, steps_g, alog_g, skip_g, bias_g = pullback(flat_grad)
            outputs_low = outputs.astype(jnp.bfloat16)
            partial_value = lax.dot_general(upstream_block, outputs_low, (((0,), (0,)), ((), ())), preferred_element_type=jnp.float32)
            weight_acc, head_acc = running
            head_acc = head_acc + jnp.stack([alog_g, skip_g, bias_g])
            return ((weight_acc + partial_value, head_acc), (inner_g, pairs_g, steps_g))
        start_sums = (jnp.zeros((D, slot_width), jnp.float32), jnp.zeros((3, HMAX), jnp.float32))
        (weight_sum, head_sum), (inner_g, pairs_g, steps_g) = lax.scan(per_block, start_sums, jnp.arange(N_DP, dtype=jnp.int32))
        inner_g = inner_g.reshape(TOKENS, slot_width)
        pairs_g = pairs_g.reshape(TOKENS, 2 * N)
        steps_g = jnp.transpose(steps_g, (1, 0, 2)).reshape(HMAX, TOKENS)
        return (weight_sum, head_sum, inner_g, pairs_g, steps_g)
    weight_all, head_all, inner_all, pairs_all, steps_all = lax.map(per_rank, ranks)
    weight_grad = jnp.transpose(weight_all, (1, 0, 2)).reshape(D, N_TENSOR * slot_width)
    head_grads = jnp.transpose(head_all, (1, 0, 2)).reshape(3, N_TENSOR * HMAX)
    inner_grad = jnp.transpose(inner_all, (1, 0, 2)).reshape(TOKENS, N_TENSOR * slot_width)
    groups_grad = jnp.transpose(pairs_all, (1, 0, 2)).reshape(TOKENS, N_TENSOR * 2 * N)
    dt_grad = steps_all.reshape(N_TENSOR * HMAX, TOKENS)
    return (inner_grad, groups_grad, dt_grad, weight_grad, head_grads)
```

```python
import functools

import jax
import jax.numpy as jnp
from jax import lax
from jax.experimental import pallas as pl
from jax.experimental.pallas import tpu as pltpu
from jax.sharding import PartitionSpec as P

MESH = pl.DeviceIdType.MESH
HIGHEST = lax.Precision.HIGHEST
F32 = jnp.float32
BF16 = jnp.bfloat16

T = 256
HALF = 128
HEADS = 10
PW = 64
WIDTH = HEADS * PW
NSTATE = 256
D = 8192
NDP = 16
NT = 16
NZ = 8
DROWS = D // NDP
AH = D // 2
NT_DIMS = (((1,), (1,)), ((), ()))

KINDS = {
    "M1+": ("u", 1, (0, 0), None),
    "M1-": ("u", -1, (0, 0), None),
    "M2+": ("u", 1, (-1, 0), 0),
    "M2-": ("u", -1, (1, 0), 1),
    "N1+": ("v", 1, (0, 0), None),
    "N1-": ("v", -1, (0, 0), None),
    "N2+": ("v", 1, (-1, 0), None),
    "N2-": ("v", -1, (-1, 0), None),
    "N3+": ("v", 1, (1, 0), None),
    "N3-": ("v", -1, (1, 0), None),
    "N4+": ("v", 1, (2, 0), 0),
    "N4-": ("v", -1, (2, 0), 0),
    "N5+": ("v", 1, (2, 0), 1),
    "N5-": ("v", -1, (2, 0), 1),
    "F1+": ("v", 1, (0, -1), 0),
    "F1-": ("v", -1, (0, 1), 1),
    "F2+": ("v", 1, (-1, -1), 0),
    "F2-": ("v", -1, (-1, 1), 1),
    "F3+": ("v", 1, (1, -1), 0),
    "F3-": ("v", -1, (1, 1), 1),
    "F4+": ("v", 1, (2, -1), 0),
    "F5-": ("v", -1, (2, 1), 1),
}
NAMES = list(KINDS)
NK = len(NAMES)


def remote(src, dst, send_sem, recv_sem, device):
    return pltpu.make_async_remote_copy(
        src_ref=src, dst_ref=dst, send_sem=send_sem, recv_sem=recv_sem, device_id=device, device_id_type=MESH
    )


def split(value):
    high = value.astype(BF16)
    return high, (value - high.astype(F32)).astype(BF16)


def dot(a, b):
    return jnp.dot(a, b, preferred_element_type=F32)


def dot_nt(a, b, precision=None):
    return lax.dot_general(a, b, NT_DIMS, precision=precision, preferred_element_type=F32)


def kernel(
    alog_ref, skip_ref, bias_ref, counts_ref, dtraw_ref, up_ref, w_ref, inner_ref, groups_ref,
    ig_ref, gg_ref, dtg_ref, wg_ref, hg_ref,
    a_buf, b_buf, bst, outs, w_buf, x_buf, bc_buf, rows, cols, pack, score, score_t, yscan, fgrad, dgt, xd, gy, gx, hbuf,
    a_send, a_recv, b_send, b_recv, s_send, s_recv, z_send, z_recv, c_send, c_recv, h_send, h_recv, local,
):
    i = lax.axis_index("dp")
    j = lax.axis_index("tensor")
    z, core = i // 2, i % 2
    y, x = j // 4, j % 4
    pending = []

    up_copy = pltpu.make_async_copy(up_ref, a_buf.at[j], local.at[0])
    up_copy.start()
    in_copy = pltpu.make_async_copy(inner_ref, x_buf, local.at[1])
    in_copy.start()
    bc_copy = pltpu.make_async_copy(groups_ref, bc_buf, local.at[2])
    bc_copy.start()
    w_copy = pltpu.make_async_copy(w_ref, w_buf, local.at[3])
    w_copy.start()

    barrier = pltpu.get_barrier_semaphore()
    peers = [((i + r) % NDP, j) for r in range(1, NDP)]
    peers += [(i, y * 4 + (x + s) % 4) for s in (1, -1)] + [(i, (y + s) % 4 * 4 + x) for s in (1, -1)]
    for peer in peers:
        pl.semaphore_signal(barrier, inc=1, device_id=peer, device_id_type=MESH)

    def slot_of(p, du, dv):
        if p == 0:
            return (y + dv) % 4 * 4 + (x + du) % 4
        return (y + du) % 4 * 4 + (x + dv) % 4

    def part(which, slot, p, q):
        if which == "a":
            size = AH if q is None else AH // 2
            return a_buf.at[slot, :, pl.ds(p * AH + (q or 0) * (AH // 2), size)]
        size = T if q is None else T // 2
        return b_buf.at[slot, pl.ds(p * T + (q or 0) * (T // 2), size), :]

    sems = {"a": (a_send, a_recv), "b": (b_send, b_recv)}

    def message(which, p, name, incoming):
        axis, way, (du, dv), q = KINDS[name]
        if incoming:
            du, dv = (du - way, dv) if axis == "u" else (du, dv - way)
        region = part(which, slot_of(p, du, dv), p, q)
        device = (i, slot_of(p, way, 0) if axis == "u" else slot_of(p, 0, way))
        send, recv = sems[which]
        k = p * NK + NAMES.index(name)
        return remote(region, region, send.at[k], recv.at[k], device)

    def send(which, *names):
        for name in names:
            for p in range(2):
                copy = message(which, p, name, False)
                copy.start()
                pending.append(copy)

    def wait(which, *names):
        for name in names:
            for p in range(2):
                message(which, p, name, True).wait_recv()

    def stage(which, step):
        if step == 0:
            send(which, "M1+", "M1-", "N1+", "N1-")
        elif step == 1:
            wait(which, "M1+", "M1-")
            send(which, "M2+", "M2-", "N2+", "N2-", "N3+", "N3-")
        elif step == 2:
            wait(which, "M2+", "M2-")
            send(which, "N4+", "N4-", "N5+", "N5-")
            wait(which, "N1+", "N1-")
            send(which, "F1+", "F1-")
        elif step == 3:
            wait(which, "N2+", "N2-", "N3+", "N3-")
            send(which, "F2+", "F2-", "F3+", "F3-")
        elif step == 4:
            wait(which, "N4+", "N4-", "N5+", "N5-")
            send(which, "F4+", "F5-")
        else:
            wait(which, "F1+", "F1-", "F2+", "F2-", "F3+", "F3-", "F4+", "F5-")

    def ring_region(dz, c, q):
        slot = (z + dz) % NZ * 2 + c
        if q is None:
            return outs.at[slot]
        return outs.at[slot, pl.ds(q * HALF, HALF), :]

    def ring(k, way, incoming):
        q = None if k < 3 else (0 if way == 1 else 1)
        dz = -way * k - (way if incoming else 0)
        region = ring_region(dz, core, q)
        n = k * 2 + (way + 1) // 2
        return remote(region, region, z_send.at[n], z_recv.at[n], ((z + way) % NZ * 2 + core, j))

    def cross(k, way, incoming):
        q = None if k < 4 else (0 if way == 1 else 1)
        region = ring_region(-way * k, 1 - core if incoming else core, q)
        n = 0 if k == 0 else k * 2 - 1 + (way + 1) // 2
        return remote(region, region, c_send.at[n], c_recv.at[n], (z * 2 + 1 - core, j))

    def ring_stage(step):
        if step > 0:
            for way in (1, -1):
                ring(step - 1, way, True).wait_recv()
        copies = []
        if step < 4:
            copies += [ring(step, way, False) for way in (1, -1)]
        copies += [cross(step, way, False) for way in ((1, -1) if step > 0 else (1,))]
        for copy in copies:
            copy.start()
            pending.append(copy)

    def cross_waits():
        cross(0, 1, True).wait_recv()
        for k in range(1, 5):
            for way in (1, -1):
                cross(k, way, True).wait_recv()

    def swap(r, incoming):
        there = (i - r) % NDP if incoming else (i + r) % NDP
        src = a_buf.at[j, :, pl.ds(pl.multiple_of((i + r) % NDP * DROWS, DROWS), DROWS)]
        return remote(src, bst.at[there if incoming else i], s_send.at[r], s_recv.at[r], ((i + r) % NDP, j))

    def heads_swap(r, incoming):
        there = (i - r) % NDP if incoming else (i + r) % NDP
        return remote(
            hbuf.at[i], hbuf.at[there if incoming else i], h_send.at[r], h_recv.at[r], ((i + r) % NDP, j)
        )

    up_copy.wait()
    pl.semaphore_wait(barrier, len(peers))
    stage("a", 0)
    for r in range(1, NDP):
        copy = swap(r, False)
        copy.start()
        pending.append(copy)
    own = pltpu.make_async_copy(
        a_buf.at[j, :, pl.ds(pl.multiple_of(i * DROWS, DROWS), DROWS)], bst.at[i], local.at[4]
    )
    own.start()

    row16 = lax.broadcasted_iota(jnp.int32, (16, T), 0)

    def fill(ref):
        out = jnp.zeros((16, T), F32)
        for h in range(HEADS):
            out = jnp.where(row16 == h, ref[h], out)
        return out

    rows[0] = jnp.zeros((16, T), F32)
    rows[0, 0:HEADS, :] = dtraw_ref[...]
    shifted = rows[0] + fill(bias_ref)
    dt = jnp.maximum(shifted, 0.0) + jnp.log1p(jnp.exp(-jnp.abs(shifted)))
    slope = 1.0 / (1.0 + jnp.exp(-shifted))
    decay = jnp.exp(fill(alog_ref))
    first = lax.broadcasted_iota(jnp.int32, (T, T), 0)
    second = lax.broadcasted_iota(jnp.int32, (T, T), 1)
    total = jnp.dot(
        dt * decay, jnp.where(first <= second, 1.0, 0.0), precision=HIGHEST, preferred_element_type=F32
    )
    rows[0] = total
    rows[1] = dt
    rows[2] = slope
    rows[3] = decay
    pack[...] = jnp.zeros((HALF, T), F32)
    pack[0:16, :] = total
    pack[16:32, :] = dt
    cols[...] = jnp.transpose(pack[...])

    in_copy.wait()
    bc_copy.wait()
    score[...] = dot_nt(bc_buf[:, NSTATE:], bc_buf[:, :NSTATE])
    score_t[...] = dot_nt(bc_buf[:, :NSTATE], bc_buf[:, NSTATE:])

    used = counts_ref[j]
    left = lax.broadcasted_iota(jnp.int32, (1, HALF), 1) < PW

    def per_lane(value, pair):
        return jnp.where(left, value(2 * pair), value(2 * pair + 1))

    def active(h):
        return jnp.where(h < used, 1.0, 0.0).astype(F32)

    def causal(rows_n, cols_n, row_start, col_start, lower):
        a = lax.broadcasted_iota(jnp.int32, (rows_n, cols_n), 0) + row_start
        b = lax.broadcasted_iota(jnp.int32, (rows_n, cols_n), 1) + col_start
        return a >= b if lower else a <= b

    def forward_pair(pair):
        lanes = slice(pair * HALF, (pair + 1) * HALF)
        values = x_buf[:, lanes]
        lane_skip = per_lane(lambda h: skip_ref[h], pair)
        lane_active = per_lane(active, pair)
        for block in range(2):
            end = (block + 1) * HALF
            here = slice(block * HALF, end)
            sides = []
            for h in (2 * pair, 2 * pair + 1):
                gap = rows[0, h : h + 1, 0:end] - cols[here, h : h + 1]
                gap = jnp.where(causal(HALF, end, block * HALF, 0, True), gap, -1e30)
                weights = jnp.exp(gap) * (score[here, 0:end] * rows[1, h : h + 1, 0:end])
                high, low = split(weights)
                sides.append(dot(high, values[0:end]) + dot(low, values[0:end]))
            scanned = jnp.where(left, sides[0], sides[1])
            yscan[here, lanes] = scanned
            out = (scanned + lane_skip * values[here].astype(F32)) * lane_active
            outs[i, here, lanes] = out.astype(BF16)

    forward_pair(0)
    forward_pair(1)
    stage("a", 1)
    forward_pair(2)
    forward_pair(3)
    forward_pair(4)
    ring_stage(0)
    stage("a", 2)

    own.wait()
    for r in range(1, NDP):
        swap(r, True).wait_recv()
    b_buf[j] = jnp.transpose(bst[...].reshape(NDP * 16, DROWS))
    stage("a", 3)
    ring_stage(1)
    stage("a", 4)
    stage("b", 0)
    w_copy.wait()
    stage("a", 5)

    depth = 1024

    def first_matmul(step, carry):
        at = pl.multiple_of(step * depth, depth)
        block = a_buf[:, :, pl.ds(at, depth)].reshape(T, depth)
        fgrad[...] += dot(block, w_buf[pl.ds(at, depth), :])
        return carry

    fgrad[...] = jnp.zeros((T, WIDTH), F32)
    lax.fori_loop(0, D // depth // 2, first_matmul, 0)
    stage("b", 1)
    lax.fori_loop(D // depth // 2, D // depth, first_matmul, 0)
    ring_stage(2)

    dgt[...] = jnp.zeros((T, T), F32)

    def backward_pair(pair):
        lanes = slice(pair * HALF, (pair + 1) * HALF)
        values = x_buf[:, lanes]
        lane_skip = per_lane(lambda h: skip_ref[h], pair)
        grad = fgrad[:, lanes] * per_lane(active, pair)
        g_high, g_low = split(grad)
        both = jnp.concatenate([g_high, g_low], axis=1)
        for block in range(2):
            start = block * HALF
            here = slice(start, start + HALF)
            sides = []
            for side, h in enumerate((2 * pair, 2 * pair + 1)):
                gap = cols[here, h : h + 1] - rows[0, h : h + 1, start:]
                gap = jnp.where(causal(HALF, T - start, start, start, False), gap, -1e30)
                scale = jnp.exp(gap) * cols[here, 16 + h : 17 + h]
                high, low = split(scale * score_t[here, start:])
                two = dot(high, both[start:])
                sides.append(two[:, :HALF] + two[:, HALF:] + dot(low, g_high[start:]))
                mine = jnp.where(left if side == 0 else jnp.logical_not(left), values[here], jnp.zeros((), BF16))
                outer = dot_nt(jnp.concatenate([mine, mine], axis=1), both[start:])
                dgt[here, start:] += scale * outer
            scanned = jnp.where(left, sides[0], sides[1])
            g_here = grad[here]
            x_here = values[here].astype(F32)
            ig_ref[here, lanes] = (scanned + lane_skip * g_here).astype(BF16)
            xd[here, lanes] = x_here * scanned
            gy[here, lanes] = g_here * yscan[here, lanes]
            gx[here, lanes] = g_here * x_here

    backward_pair(0)
    backward_pair(1)
    stage("b", 2)
    backward_pair(2)
    ring_stage(3)
    backward_pair(3)
    backward_pair(4)
    stage("b", 3)

    head_of = lax.broadcasted_iota(jnp.int32, (16, WIDTH), 1) // PW
    pick = jnp.where(head_of == lax.broadcasted_iota(jnp.int32, (16, WIDTH), 0), 1.0, 0.0)
    entry_sum = dot_nt(pick, xd[...], HIGHEST)
    exit_sum = dot_nt(pick, gy[...], HIGHEST)
    skip_sum = dot_nt(pick, gx[...], HIGHEST)
    rate_grad = jnp.dot(
        entry_sum - exit_sum,
        jnp.where(first >= second, 1.0, 0.0),
        precision=HIGHEST,
        preferred_element_type=F32,
    )
    dt_now, decay_now = rows[1], rows[3]
    raw_grad = (entry_sum / dt_now + rate_grad * decay_now) * rows[2]
    dtg_ref[...] = raw_grad[0:HEADS, :]
    alog_part = jnp.sum(rate_grad * dt_now * decay_now, axis=1, keepdims=True)
    skip_part = jnp.sum(skip_sum, axis=1, keepdims=True)
    bias_part = jnp.sum(raw_grad, axis=1, keepdims=True)
    lane16 = lax.broadcasted_iota(jnp.int32, (16, HALF), 1)
    hbuf[i] = jnp.where(
        lane16 == 0, alog_part, jnp.where(lane16 == 1, skip_part, jnp.where(lane16 == 2, bias_part, 0.0))
    )
    for r in range(1, NDP):
        copy = heads_swap(r, False)
        copy.start()
        pending.append(copy)

    low_high, low_low = split(dgt[...])
    gg_ref[:, :NSTATE] = (dot(low_high, bc_buf[:, NSTATE:]) + dot(low_low, bc_buf[:, NSTATE:])).astype(BF16)
    up_high, up_low = split(jnp.transpose(dgt[...]))
    gg_ref[:, NSTATE:] = (dot(up_high, bc_buf[:, :NSTATE]) + dot(up_low, bc_buf[:, :NSTATE])).astype(BF16)

    ring_stage(4)
    stage("b", 4)
    cross_waits()

    def second_matmul(dv):
        for p in range(2):
            slots = [slot_of(p, du, dv) for du in range(4)]
            left_side = jnp.concatenate([b_buf[s, p * T : (p + 1) * T, :] for s in slots], axis=1)
            right_side = jnp.concatenate(
                [outs[:, pl.ds(pl.multiple_of(s * 16, 16), 16), :].reshape(T, WIDTH) for s in slots], axis=0
            )
            here = slice(p * T, (p + 1) * T)
            if dv == 0:
                wg_ref[here, :] = dot(left_side, right_side)
            else:
                wg_ref[here, :] += dot(left_side, right_side)

    second_matmul(0)
    second_matmul(1)
    second_matmul(-1)
    for r in range(1, NDP):
        heads_swap(r, True).wait_recv()
    tot = hbuf[0]
    for r in range(1, NDP):
        tot = tot + hbuf[r]
    eye = jnp.where(
        lax.broadcasted_iota(jnp.int32, (8, HALF), 0) == lax.broadcasted_iota(jnp.int32, (8, HALF), 1), 1.0, 0.0
    )
    hg_ref[...] = dot_nt(eye, tot, HIGHEST)[0:3, 0:HEADS]
    stage("b", 5)
    second_matmul(2)
    for copy in pending:
        copy.wait_send()


def body(upstream, out_weight, inner, groups_bc, dt_raw, a_log, skip, dt_bias, head_counts):
    smem = pl.BlockSpec(memory_space=pltpu.SMEM)
    vmem = pl.BlockSpec(memory_space=pltpu.VMEM)
    hbm = pl.BlockSpec(memory_space=pl.ANY)
    dma = lambda n: pltpu.SemaphoreType.DMA((n,))
    return pl.pallas_call(
        kernel,
        out_shape=(
            jax.ShapeDtypeStruct((T, WIDTH), BF16),
            jax.ShapeDtypeStruct((T, 2 * NSTATE), BF16),
            jax.ShapeDtypeStruct((HEADS, T), F32),
            jax.ShapeDtypeStruct((DROWS, WIDTH), F32),
            jax.ShapeDtypeStruct((3, HEADS), F32),
        ),
        in_specs=[smem] * 4 + [vmem] + [hbm] * 4,
        out_specs=(vmem,) * 5,
        scratch_shapes=[
            pltpu.VMEM((NT, 16, D), BF16),
            pltpu.VMEM((NT, DROWS, T), BF16),
            pltpu.VMEM((NDP, 16, DROWS), BF16),
            pltpu.VMEM((NDP, T, WIDTH), BF16),
            pltpu.VMEM((D, WIDTH), BF16),
            pltpu.VMEM((T, WIDTH), BF16),
            pltpu.VMEM((T, 2 * NSTATE), BF16),
            pltpu.VMEM((4, 16, T), F32),
            pltpu.VMEM((T, HALF), F32),
            pltpu.VMEM((HALF, T), F32),
            pltpu.VMEM((T, T), F32),
            pltpu.VMEM((T, T), F32),
            pltpu.VMEM((T, WIDTH), F32),
            pltpu.VMEM((T, WIDTH), F32),
            pltpu.VMEM((T, T), F32),
            pltpu.VMEM((T, WIDTH), F32),
            pltpu.VMEM((T, WIDTH), F32),
            pltpu.VMEM((T, WIDTH), F32),
            pltpu.VMEM((NDP, 16, HALF), F32),
            dma(2 * NK), dma(2 * NK), dma(2 * NK), dma(2 * NK),
            dma(NDP), dma(NDP), dma(8), dma(8), dma(9), dma(9), dma(NDP), dma(NDP), dma(5),
        ],
        compiler_params=pltpu.CompilerParams(
            collective_id=0, has_side_effects=True, vmem_limit_bytes=56 * 1024 * 1024
        ),
    )(a_log, skip, dt_bias, head_counts, dt_raw, upstream, out_weight, inner, groups_bc)


def solution(mesh):
    return jax.shard_map(
        body,
        mesh=mesh,
        in_specs=(
            P(("dp", "tensor"), None),
            P(None, "tensor"),
            P("dp", "tensor"),
            P("dp", "tensor"),
            P("tensor", "dp"),
            P("tensor"),
            P("tensor"),
            P("tensor"),
            P(),
        ),
        out_specs=(
            P("dp", "tensor"),
            P("dp", "tensor"),
            P("tensor", "dp"),
            P("dp", "tensor"),
            P(None, "tensor"),
        ),
        check_vma=False,
    )
```

```python
import functools

import jax
import jax.numpy as jnp
from jax import lax
from jax.experimental import pallas as pl
from jax.experimental.pallas import tpu as pltpu
from jax.sharding import PartitionSpec as P

MESH = pl.DeviceIdType.MESH
HIGHEST = lax.Precision.HIGHEST
F32 = jnp.float32
BF16 = jnp.bfloat16

T = 256
HALF = 128
HEADS = 10
PW = 64
WIDTH = HEADS * PW
NSTATE = 256
D = 8192
NDP = 16
NT = 16
NZ = 8
DROWS = D // NDP
AH = D // 2
NT_DIMS = (((1,), (1,)), ((), ()))

KINDS = {
    "M1+": ("u", 1, (0, 0), None),
    "M1-": ("u", -1, (0, 0), None),
    "M2+": ("u", 1, (-1, 0), 0),
    "M2-": ("u", -1, (1, 0), 1),
    "N1+": ("v", 1, (0, 0), None),
    "N1-": ("v", -1, (0, 0), None),
    "N2+": ("v", 1, (-1, 0), None),
    "N2-": ("v", -1, (-1, 0), None),
    "N3+": ("v", 1, (1, 0), None),
    "N3-": ("v", -1, (1, 0), None),
    "N4+": ("v", 1, (2, 0), 0),
    "N4-": ("v", -1, (2, 0), 0),
    "N5+": ("v", 1, (2, 0), 1),
    "N5-": ("v", -1, (2, 0), 1),
    "F1+": ("v", 1, (0, -1), 0),
    "F1-": ("v", -1, (0, 1), 1),
    "F2+": ("v", 1, (-1, -1), 0),
    "F2-": ("v", -1, (-1, 1), 1),
    "F3+": ("v", 1, (1, -1), 0),
    "F3-": ("v", -1, (1, 1), 1),
    "F4+": ("v", 1, (2, -1), 0),
    "F5-": ("v", -1, (2, 1), 1),
}
NAMES = list(KINDS)
NK = len(NAMES)


def remote(src, dst, send_sem, recv_sem, device):
    return pltpu.make_async_remote_copy(
        src_ref=src, dst_ref=dst, send_sem=send_sem, recv_sem=recv_sem, device_id=device, device_id_type=MESH
    )


def split(value):
    high = value.astype(BF16)
    return high, (value - high.astype(F32)).astype(BF16)


def dot(a, b):
    return jnp.dot(a, b, preferred_element_type=F32)


def dot_nt(a, b, precision=None):
    return lax.dot_general(a, b, NT_DIMS, precision=precision, preferred_element_type=F32)


def kernel(
    alog_ref, skip_ref, bias_ref, counts_ref, dtraw_ref, up_ref, w_ref, inner_ref, groups_ref,
    ig_ref, gg_ref, dtg_ref, wg_ref, hg_ref,
    a_buf, b_buf, bst, outs, w_buf, x_buf, bc_buf, rows, cols, pack, score, score_t, yscan, fgrad, dgt, xd, gy, gx, hbuf,
    a_send, a_recv, b_send, b_recv, s_send, s_recv, z_send, z_recv, c_send, c_recv, h_send, h_recv, local,
):
    i = lax.axis_index("dp")
    j = lax.axis_index("tensor")
    z, core = i // 2, i % 2
    y, x = j // 4, j % 4
    pending = []

    up_copy = pltpu.make_async_copy(up_ref, a_buf.at[j], local.at[0])
    up_copy.start()
    in_copy = pltpu.make_async_copy(inner_ref, x_buf, local.at[1])
    in_copy.start()
    bc_copy = pltpu.make_async_copy(groups_ref, bc_buf, local.at[2])
    bc_copy.start()
    w_copy = pltpu.make_async_copy(w_ref, w_buf, local.at[3])
    w_copy.start()

    barrier = pltpu.get_barrier_semaphore()
    peers = [((i + r) % NDP, j) for r in range(1, NDP)]
    peers += [(i, y * 4 + (x + s) % 4) for s in (1, -1)] + [(i, (y + s) % 4 * 4 + x) for s in (1, -1)]
    for peer in peers:
        pl.semaphore_signal(barrier, inc=1, device_id=peer, device_id_type=MESH)

    def slot_of(p, du, dv):
        if p == 0:
            return (y + dv) % 4 * 4 + (x + du) % 4
        return (y + du) % 4 * 4 + (x + dv) % 4

    def part(which, slot, p, q):
        if which == "a":
            size = AH if q is None else AH // 2
            return a_buf.at[slot, :, pl.ds(p * AH + (q or 0) * (AH // 2), size)]
        size = T if q is None else T // 2
        return b_buf.at[slot, pl.ds(p * T + (q or 0) * (T // 2), size), :]

    sems = {"a": (a_send, a_recv), "b": (b_send, b_recv)}

    def message(which, p, name, incoming):
        axis, way, (du, dv), q = KINDS[name]
        if incoming:
            du, dv = (du - way, dv) if axis == "u" else (du, dv - way)
        region = part(which, slot_of(p, du, dv), p, q)
        device = (i, slot_of(p, way, 0) if axis == "u" else slot_of(p, 0, way))
        send, recv = sems[which]
        k = p * NK + NAMES.index(name)
        return remote(region, region, send.at[k], recv.at[k], device)

    def send(which, *names):
        for name in names:
            for p in range(2):
                copy = message(which, p, name, False)
                copy.start()
                pending.append(copy)

    def wait(which, *names):
        for name in names:
            for p in range(2):
                message(which, p, name, True).wait_recv()

    def stage(which, step):
        if step == 0:
            send(which, "M1+", "M1-", "N1+", "N1-")
        elif step == 1:
            wait(which, "M1+", "M1-")
            send(which, "M2+", "M2-", "N2+", "N2-", "N3+", "N3-")
        elif step == 2:
            wait(which, "M2+", "M2-")
            send(which, "N4+", "N4-", "N5+", "N5-")
            wait(which, "N1+", "N1-")
            send(which, "F1+", "F1-")
        elif step == 3:
            wait(which, "N2+", "N2-", "N3+", "N3-")
            send(which, "F2+", "F2-", "F3+", "F3-")
        elif step == 4:
            wait(which, "N4+", "N4-", "N5+", "N5-")
            send(which, "F4+", "F5-")
        else:
            wait(which, "F1+", "F1-", "F2+", "F2-", "F3+", "F3-", "F4+", "F5-")

    def ring_region(dz, c, q):
        return outs.at[(z + dz) % NZ * 2 + c, pl.ds(q * HALF, HALF), :]

    def ring(k, way, q, incoming):
        region = ring_region(-way * k - (way if incoming else 0), core, q)
        n = (k * 2 + q) * 2 + (way + 1) // 2
        return remote(region, region, z_send.at[n], z_recv.at[n], ((z + way) % NZ * 2 + core, j))

    def cross(k, way, q, incoming):
        region = ring_region(-way * k, 1 - core if incoming else core, q)
        n = (k * 2 + q) * 2 + (way + 1) // 2
        return remote(region, region, c_send.at[n], c_recv.at[n], (z * 2 + 1 - core, j))

    def goes(k, way, q):
        return k < 3 or q == (0 if way == 1 else 1)

    def ring_stage(step, q):
        for way in (1, -1):
            if step > 0:
                if not goes(step - 1, way, q):
                    continue
                ring(step - 1, way, q, True).wait_recv()
            copies = []
            if step < 4 and goes(step, way, q):
                copies.append(ring(step, way, q, False))
            if step > 0 or way == 1:
                copies.append(cross(step, way, q, False))
            for copy in copies:
                copy.start()
                pending.append(copy)

    def cross_waits():
        for q in range(2):
            cross(0, 1, q, True).wait_recv()
            for k in range(1, 5):
                for way in (1, -1):
                    if goes(k - 1, way, q):
                        cross(k, way, q, True).wait_recv()

    def swap(r, incoming):
        there = (i - r) % NDP if incoming else (i + r) % NDP
        src = a_buf.at[j, :, pl.ds(pl.multiple_of((i + r) % NDP * DROWS, DROWS), DROWS)]
        return remote(src, bst.at[there if incoming else i], s_send.at[r], s_recv.at[r], ((i + r) % NDP, j))

    def heads_swap(r, incoming):
        there = (i - r) % NDP if incoming else (i + r) % NDP
        return remote(
            hbuf.at[i], hbuf.at[there if incoming else i], h_send.at[r], h_recv.at[r], ((i + r) % NDP, j)
        )

    up_copy.wait()
    pl.semaphore_wait(barrier, len(peers))
    stage("a", 0)
    for r in range(1, NDP):
        copy = swap(r, False)
        copy.start()
        pending.append(copy)
    own = pltpu.make_async_copy(
        a_buf.at[j, :, pl.ds(pl.multiple_of(i * DROWS, DROWS), DROWS)], bst.at[i], local.at[4]
    )
    own.start()

    row16 = lax.broadcasted_iota(jnp.int32, (16, T), 0)

    def fill(ref):
        out = jnp.zeros((16, T), F32)
        for h in range(HEADS):
            out = jnp.where(row16 == h, ref[h], out)
        return out

    rows[0] = jnp.zeros((16, T), F32)
    rows[0, 0:HEADS, :] = dtraw_ref[...]
    shifted = rows[0] + fill(bias_ref)
    dt = jnp.maximum(shifted, 0.0) + jnp.log1p(jnp.exp(-jnp.abs(shifted)))
    slope = 1.0 / (1.0 + jnp.exp(-shifted))
    decay = jnp.exp(fill(alog_ref))
    first = lax.broadcasted_iota(jnp.int32, (T, T), 0)
    second = lax.broadcasted_iota(jnp.int32, (T, T), 1)
    total = jnp.dot(
        dt * decay, jnp.where(first <= second, 1.0, 0.0), precision=HIGHEST, preferred_element_type=F32
    )
    rows[0] = total
    rows[1] = dt
    rows[2] = slope
    rows[3] = decay
    pack[...] = jnp.zeros((HALF, T), F32)
    pack[0:16, :] = total
    pack[16:32, :] = dt
    cols[...] = jnp.transpose(pack[...])

    in_copy.wait()
    bc_copy.wait()
    score[...] = dot_nt(bc_buf[:, NSTATE:], bc_buf[:, :NSTATE])
    score_t[...] = dot_nt(bc_buf[:, :NSTATE], bc_buf[:, NSTATE:])

    used = counts_ref[j]
    left = lax.broadcasted_iota(jnp.int32, (1, HALF), 1) < PW

    def per_lane(value, pair):
        return jnp.where(left, value(2 * pair), value(2 * pair + 1))

    def active(h):
        return jnp.where(h < used, 1.0, 0.0).astype(F32)

    def causal(rows_n, cols_n, row_start, col_start, lower):
        a = lax.broadcasted_iota(jnp.int32, (rows_n, cols_n), 0) + row_start
        b = lax.broadcasted_iota(jnp.int32, (rows_n, cols_n), 1) + col_start
        return a >= b if lower else a <= b

    def forward_pair(pair):
        lanes = slice(pair * HALF, (pair + 1) * HALF)
        values = x_buf[:, lanes]
        lane_skip = per_lane(lambda h: skip_ref[h], pair)
        lane_active = per_lane(active, pair)
        for block in range(2):
            end = (block + 1) * HALF
            here = slice(block * HALF, end)
            sides = []
            for h in (2 * pair, 2 * pair + 1):
                gap = rows[0, h : h + 1, 0:end] - cols[here, h : h + 1]
                gap = jnp.where(causal(HALF, end, block * HALF, 0, True), gap, -1e30)
                weights = jnp.exp(gap) * (score[here, 0:end] * rows[1, h : h + 1, 0:end])
                high, low = split(weights)
                sides.append(dot(high, values[0:end]) + dot(low, values[0:end]))
            scanned = jnp.where(left, sides[0], sides[1])
            yscan[here, lanes] = scanned
            out = (scanned + lane_skip * values[here].astype(F32)) * lane_active
            outs[i, here, lanes] = out.astype(BF16)

    forward_pair(0)
    forward_pair(1)
    stage("a", 1)
    forward_pair(2)
    forward_pair(3)
    forward_pair(4)
    ring_stage(0, 0)
    ring_stage(0, 1)
    stage("a", 2)

    own.wait()
    for r in range(1, NDP):
        swap(r, True).wait_recv()
    b_buf[j] = jnp.transpose(bst[...].reshape(NDP * 16, DROWS))
    stage("a", 3)
    ring_stage(1, 0)
    stage("a", 4)
    stage("b", 0)
    ring_stage(1, 1)
    w_copy.wait()
    ring_stage(2, 0)
    stage("a", 5)

    depth = 1024

    def first_matmul(step, carry):
        at = pl.multiple_of(step * depth, depth)
        block = a_buf[:, :, pl.ds(at, depth)].reshape(T, depth)
        fgrad[...] += dot(block, w_buf[pl.ds(at, depth), :])
        return carry

    fgrad[...] = jnp.zeros((T, WIDTH), F32)
    lax.fori_loop(0, D // depth // 2, first_matmul, 0)
    ring_stage(2, 1)
    lax.fori_loop(D // depth // 2, D // depth, first_matmul, 0)
    stage("b", 1)

    dgt[...] = jnp.zeros((T, T), F32)

    def backward_pair(pair):
        lanes = slice(pair * HALF, (pair + 1) * HALF)
        values = x_buf[:, lanes]
        lane_skip = per_lane(lambda h: skip_ref[h], pair)
        grad = fgrad[:, lanes] * per_lane(active, pair)
        g_high, g_low = split(grad)
        both = jnp.concatenate([g_high, g_low], axis=1)
        for block in range(2):
            start = block * HALF
            here = slice(start, start + HALF)
            sides = []
            for side, h in enumerate((2 * pair, 2 * pair + 1)):
                gap = cols[here, h : h + 1] - rows[0, h : h + 1, start:]
                gap = jnp.where(causal(HALF, T - start, start, start, False), gap, -1e30)
                scale = jnp.exp(gap) * cols[here, 16 + h : 17 + h]
                high, low = split(scale * score_t[here, start:])
                two = dot(high, both[start:])
                sides.append(two[:, :HALF] + two[:, HALF:] + dot(low, g_high[start:]))
                mine = jnp.where(left if side == 0 else jnp.logical_not(left), values[here], jnp.zeros((), BF16))
                outer = dot_nt(jnp.concatenate([mine, mine], axis=1), both[start:])
                dgt[here, start:] += scale * outer
            scanned = jnp.where(left, sides[0], sides[1])
            g_here = grad[here]
            x_here = values[here].astype(F32)
            ig_ref[here, lanes] = (scanned + lane_skip * g_here).astype(BF16)
            xd[here, lanes] = x_here * scanned
            gy[here, lanes] = g_here * yscan[here, lanes]
            gx[here, lanes] = g_here * x_here

    backward_pair(0)
    backward_pair(1)
    ring_stage(3, 0)
    backward_pair(2)
    stage("b", 2)
    backward_pair(3)
    ring_stage(3, 1)
    backward_pair(4)

    head_of = lax.broadcasted_iota(jnp.int32, (16, WIDTH), 1) // PW
    pick = jnp.where(head_of == lax.broadcasted_iota(jnp.int32, (16, WIDTH), 0), 1.0, 0.0)
    entry_sum = dot_nt(pick, xd[...], HIGHEST)
    exit_sum = dot_nt(pick, gy[...], HIGHEST)
    skip_sum = dot_nt(pick, gx[...], HIGHEST)
    rate_grad = jnp.dot(
        entry_sum - exit_sum,
        jnp.where(first >= second, 1.0, 0.0),
        precision=HIGHEST,
        preferred_element_type=F32,
    )
    dt_now, decay_now = rows[1], rows[3]
    raw_grad = (entry_sum / dt_now + rate_grad * decay_now) * rows[2]
    dtg_ref[...] = raw_grad[0:HEADS, :]
    alog_part = jnp.sum(rate_grad * dt_now * decay_now, axis=1, keepdims=True)
    skip_part = jnp.sum(skip_sum, axis=1, keepdims=True)
    bias_part = jnp.sum(raw_grad, axis=1, keepdims=True)
    lane16 = lax.broadcasted_iota(jnp.int32, (16, HALF), 1)
    hbuf[i] = jnp.where(
        lane16 == 0, alog_part, jnp.where(lane16 == 1, skip_part, jnp.where(lane16 == 2, bias_part, 0.0))
    )
    for r in range(1, NDP):
        copy = heads_swap(r, False)
        copy.start()
        pending.append(copy)

    low_high, low_low = split(dgt[...])
    gg_ref[:, :NSTATE] = (dot(low_high, bc_buf[:, NSTATE:]) + dot(low_low, bc_buf[:, NSTATE:])).astype(BF16)
    up_high, up_low = split(jnp.transpose(dgt[...]))
    gg_ref[:, NSTATE:] = (dot(up_high, bc_buf[:, :NSTATE]) + dot(up_low, bc_buf[:, :NSTATE])).astype(BF16)

    stage("b", 3)
    ring_stage(4, 0)
    ring_stage(4, 1)
    stage("b", 4)
    cross_waits()

    def second_matmul(dv):
        for p in range(2):
            slots = [slot_of(p, du, dv) for du in range(4)]
            left_side = jnp.concatenate([b_buf[s, p * T : (p + 1) * T, :] for s in slots], axis=1)
            right_side = jnp.concatenate(
                [outs[:, pl.ds(pl.multiple_of(s * 16, 16), 16), :].reshape(T, WIDTH) for s in slots], axis=0
            )
            here = slice(p * T, (p + 1) * T)
            if dv == 0:
                wg_ref[here, :] = dot(left_side, right_side)
            else:
                wg_ref[here, :] += dot(left_side, right_side)

    second_matmul(0)
    second_matmul(1)
    second_matmul(-1)
    for r in range(1, NDP):
        heads_swap(r, True).wait_recv()
    tot = hbuf[0]
    for r in range(1, NDP):
        tot = tot + hbuf[r]
    eye = jnp.where(
        lax.broadcasted_iota(jnp.int32, (8, HALF), 0) == lax.broadcasted_iota(jnp.int32, (8, HALF), 1), 1.0, 0.0
    )
    hg_ref[...] = dot_nt(eye, tot, HIGHEST)[0:3, 0:HEADS]
    stage("b", 5)
    second_matmul(2)
    for copy in pending:
        copy.wait_send()


def publish(*refs):
    sems = refs[10]
    copies = [pltpu.make_async_copy(refs[n], refs[5 + n], sems.at[n]) for n in range(5)]
    for copy in copies:
        copy.start()
    for copy in copies:
        copy.wait()


def body(upstream, out_weight, inner, groups_bc, dt_raw, a_log, skip, dt_bias, head_counts):
    smem = pl.BlockSpec(memory_space=pltpu.SMEM)
    vmem = pl.BlockSpec(memory_space=pltpu.VMEM)
    hbm = pl.BlockSpec(memory_space=pl.ANY)
    dma = lambda n: pltpu.SemaphoreType.DMA((n,))
    shapes = (
        ((T, WIDTH), BF16),
        ((T, 2 * NSTATE), BF16),
        ((HEADS, T), F32),
        ((DROWS, WIDTH), F32),
        ((3, HEADS), F32),
    )
    results = pl.pallas_call(
        kernel,
        out_shape=tuple(pltpu.VMEM(*one) for one in shapes),
        in_specs=[smem] * 4 + [vmem] + [hbm] * 4,
        out_specs=(vmem,) * 5,
        scratch_shapes=[
            pltpu.VMEM((NT, 16, D), BF16),
            pltpu.VMEM((NT, DROWS, T), BF16),
            pltpu.VMEM((NDP, 16, DROWS), BF16),
            pltpu.VMEM((NDP, T, WIDTH), BF16),
            pltpu.VMEM((D, WIDTH), BF16),
            pltpu.VMEM((T, WIDTH), BF16),
            pltpu.VMEM((T, 2 * NSTATE), BF16),
            pltpu.VMEM((4, 16, T), F32),
            pltpu.VMEM((T, HALF), F32),
            pltpu.VMEM((HALF, T), F32),
            pltpu.VMEM((T, T), F32),
            pltpu.VMEM((T, T), F32),
            pltpu.VMEM((T, WIDTH), F32),
            pltpu.VMEM((T, WIDTH), F32),
            pltpu.VMEM((T, T), F32),
            pltpu.VMEM((T, WIDTH), F32),
            pltpu.VMEM((T, WIDTH), F32),
            pltpu.VMEM((T, WIDTH), F32),
            pltpu.VMEM((NDP, 16, HALF), F32),
            dma(2 * NK), dma(2 * NK), dma(2 * NK), dma(2 * NK),
            dma(NDP), dma(NDP), dma(16), dma(16), dma(20), dma(20), dma(NDP), dma(NDP), dma(5),
        ],
        compiler_params=pltpu.CompilerParams(
            collective_id=0, has_side_effects=True, vmem_limit_bytes=56 * 1024 * 1024
        ),
    )(a_log, skip, dt_bias, head_counts, dt_raw, upstream, out_weight, inner, groups_bc)
    return pl.pallas_call(
        publish,
        out_shape=tuple(jax.ShapeDtypeStruct(*one) for one in shapes),
        in_specs=[vmem] * 5,
        out_specs=(hbm,) * 5,
        scratch_shapes=[dma(5)],
    )(*[pltpu.with_memory_space_constraint(one, pltpu.VMEM) for one in results])


def solution(mesh):
    return jax.shard_map(
        body,
        mesh=mesh,
        in_specs=(
            P(("dp", "tensor"), None),
            P(None, "tensor"),
            P("dp", "tensor"),
            P("dp", "tensor"),
            P("tensor", "dp"),
            P("tensor"),
            P("tensor"),
            P("tensor"),
            P(),
        ),
        out_specs=(
            P("dp", "tensor"),
            P("dp", "tensor"),
            P("tensor", "dp"),
            P("dp", "tensor"),
            P(None, "tensor"),
        ),
        check_vma=False,
    )
```

```python
import functools

import jax
import jax.numpy as jnp
from jax import lax
from jax.experimental import pallas as pl
from jax.experimental.pallas import tpu as pltpu
from jax.sharding import PartitionSpec as P

MESH = pl.DeviceIdType.MESH
HIGHEST = lax.Precision.HIGHEST
F32 = jnp.float32
BF16 = jnp.bfloat16

T = 256
HALF = 128
HEADS = 10
PW = 64
WIDTH = HEADS * PW
NSTATE = 256
D = 8192
NDP = 16
NT = 16
NZ = 8
DROWS = D // NDP
AH = D // 2
NT_DIMS = (((1,), (1,)), ((), ()))
TN_DIMS = (((0,), (0,)), ((), ()))

PLACES = [(dz, c) for dz in (2, 3, 5, 6) for c in (0, 1)] + [(1, 1), (7, 1), (4, 0), (4, 1)]
PLACES += [(0, 0), (0, 1), (1, 0), (7, 0)]
FAR = 12
MOST = 10
KB = FAR * 16

KINDS = {
    "M1+": ("u", 1, (0, 0), None),
    "M1-": ("u", -1, (0, 0), None),
    "M2+": ("u", 1, (-1, 0), 0),
    "M2-": ("u", -1, (1, 0), 1),
    "N1+": ("v", 1, (0, 0), None),
    "N1-": ("v", -1, (0, 0), None),
    "N2+": ("v", 1, (-1, 0), None),
    "N2-": ("v", -1, (-1, 0), None),
    "N3+": ("v", 1, (1, 0), None),
    "N3-": ("v", -1, (1, 0), None),
    "N4+": ("v", 1, (2, 0), 0),
    "N4-": ("v", -1, (2, 0), 0),
    "N5+": ("v", 1, (2, 0), 1),
    "N5-": ("v", -1, (2, 0), 1),
    "F1+": ("v", 1, (0, -1), 0),
    "F1-": ("v", -1, (0, 1), 1),
    "F2+": ("v", 1, (-1, -1), 0),
    "F2-": ("v", -1, (-1, 1), 1),
    "F3+": ("v", 1, (1, -1), 0),
    "F3-": ("v", -1, (1, 1), 1),
    "F4+": ("v", 1, (2, -1), 0),
    "F5-": ("v", -1, (2, 1), 1),
}
NAMES = list(KINDS)
NK = len(NAMES)


def remote(src, dst, send_sem, recv_sem, device):
    return pltpu.make_async_remote_copy(
        src_ref=src, dst_ref=dst, send_sem=send_sem, recv_sem=recv_sem, device_id=device, device_id_type=MESH
    )


def split(value):
    high = value.astype(BF16)
    return high, (value - high.astype(F32)).astype(BF16)


def dot(a, b):
    return jnp.dot(a, b, preferred_element_type=F32)


def dot_tn(a, b):
    return lax.dot_general(a, b, TN_DIMS, preferred_element_type=F32)


def dot_nt(a, b, precision=None):
    return lax.dot_general(a, b, NT_DIMS, precision=precision, preferred_element_type=F32)


def kernel(
    alog_hbm, skip_hbm, bias_hbm, counts_hbm, dtraw_hbm, up_ref, w_ref, inner_ref, groups_ref,
    ig_ref, gg_ref, dtg_ref, wg_ref, hg_ref,
    alog_ref, skip_ref, bias_ref, counts_ref, dtraw_ref, a_buf, b_buf, near, outs, w_buf, x_buf, bc_buf, rows, cols, pack, score, score_t, yscan, fgrad, dgt, xd, gy, gx, hbuf,
    a_send, a_recv, b_send, b_recv, s_send, s_recv, n_send, n_recv, z_send, z_recv, c_send, c_recv, h_send, h_recv, local,
):
    i = lax.axis_index("dp")
    j = lax.axis_index("tensor")
    z, core = i // 2, i % 2
    y, x = j // 4, j % 4
    pending = []

    barrier = pltpu.get_barrier_semaphore()
    peers = [(i, y * 4 + (x + s) % 4) for s in (1, -1)] + [(i, (y + s) % 4 * 4 + x) for s in (1, -1)]
    peers += [((i + r) % NDP, j) for r in range(1, NDP)]
    for peer in peers:
        pl.semaphore_signal(barrier, inc=1, device_id=peer, device_id_type=MESH)

    def fetch(n, src, dst):
        copy = pltpu.make_async_copy(src, dst, local.at[n])
        copy.start()
        return copy

    up_copy = fetch(0, up_ref, a_buf.at[j])
    small = [
        fetch(4, alog_hbm, alog_ref),
        fetch(5, skip_hbm, skip_ref),
        fetch(6, bias_hbm, bias_ref),
        fetch(7, counts_hbm, counts_ref),
        fetch(8, dtraw_hbm, dtraw_ref),
    ]
    bc_copy = fetch(2, groups_ref, bc_buf)
    in_copy = fetch(1, inner_ref, x_buf)
    w_copy = fetch(3, w_ref, w_buf)

    def slot_of(p, du, dv):
        if p == 0:
            return (y + dv) % 4 * 4 + (x + du) % 4
        return (y + du) % 4 * 4 + (x + dv) % 4

    def part(which, slot, p, q):
        if which == "a":
            size = AH if q is None else AH // 2
            return a_buf.at[slot, :, pl.ds(p * AH + (q or 0) * (AH // 2), size)]
        size = T if q is None else T // 2
        return b_buf.at[slot, :, pl.ds(p * T + (q or 0) * (T // 2), size)]

    sems = {"a": (a_send, a_recv), "b": (b_send, b_recv)}

    def message(which, p, name, incoming):
        axis, way, (du, dv), q = KINDS[name]
        if incoming:
            du, dv = (du - way, dv) if axis == "u" else (du, dv - way)
        region = part(which, slot_of(p, du, dv), p, q)
        device = (i, slot_of(p, way, 0) if axis == "u" else slot_of(p, 0, way))
        send, recv = sems[which]
        k = p * NK + NAMES.index(name)
        return remote(region, region, send.at[k], recv.at[k], device)

    def send(which, *names):
        for name in names:
            for p in range(2):
                copy = message(which, p, name, False)
                copy.start()
                pending.append(copy)

    def wait(which, *names):
        for name in names:
            for p in range(2):
                message(which, p, name, True).wait_recv()

    def stage(which, step):
        if step == 0:
            send(which, "M1+", "M1-", "N1+", "N1-")
        elif step == 1:
            wait(which, "M1+", "M1-")
            send(which, "M2+", "M2-", "N2+", "N2-", "N3+", "N3-")
        elif step == 2:
            wait(which, "M2+", "M2-")
            send(which, "N4+", "N4-", "N5+", "N5-")
            wait(which, "N1+", "N1-")
            send(which, "F1+", "F1-")
        elif step == 3:
            wait(which, "N2+", "N2-", "N3+", "N3-")
            send(which, "F2+", "F2-", "F3+", "F3-")
        elif step == 4:
            wait(which, "N4+", "N4-", "N5+", "N5-")
            send(which, "F4+", "F5-")
        else:
            wait(which, "F1+", "F1-", "F2+", "F2-", "F3+", "F3-", "F4+", "F5-")

    def place(dz, other):
        return PLACES.index((dz % NZ, other))

    def half_block(at, q):
        return outs.at[at, pl.ds(q * HALF, HALF), :]

    def ring(k, way, q, incoming):
        here, there = half_block(place(-way * k, 0), q), half_block(place(-way * (k + 1), 0), q)
        n = (k * 2 + q) * 2 + (way + 1) // 2
        return remote(
            there if incoming else here, there, z_send.at[n], z_recv.at[n], ((z + way) % NZ * 2 + core, j)
        )

    def cross(k, way, q, incoming):
        here, there = half_block(place(-way * k, 0), q), half_block(place(-way * k, 1), q)
        n = (k * 2 + q) * 2 + (way + 1) // 2
        return remote(there if incoming else here, there, c_send.at[n], c_recv.at[n], (z * 2 + 1 - core, j))

    def goes(k, way, q):
        return k < 3 or q == (0 if way == 1 else 1)

    def ring_stage(step, q):
        for way in (1, -1):
            if step > 0:
                if not goes(step - 1, way, q):
                    continue
                ring(step - 1, way, q, True).wait_recv()
            copies = []
            if step < 4 and goes(step, way, q):
                copies.append(ring(step, way, q, False))
            if step > 0 or way == 1:
                copies.append(cross(step, way, q, False))
            for copy in copies:
                copy.start()
                pending.append(copy)

    def cross_waits(hops):
        for k in hops:
            for q in range(2):
                for way in (1, -1) if k > 0 else (1,):
                    if goes(k - 1, way, q):
                        cross(k, way, q, True).wait_recv()

    def columns(dp):
        return pl.ds(pl.multiple_of(dp * DROWS, DROWS), DROWS)

    def at_place(dz, other):
        return (z + dz) % NZ * 2 + (core + other) % 2

    def swap(n, incoming):
        dz, other = PLACES[n]
        to = at_place(-dz, other)
        dst = b_buf.at[j, pl.ds(n * 16, 16), :]
        src = dst if incoming else a_buf.at[j, :, columns(to)]
        return remote(src, dst, s_send.at[n], s_recv.at[n], (to, j))

    def near_swap(n, half, incoming):
        dz, other = PLACES[FAR + 1 + n]
        to = at_place(-dz, other)
        dst = near.at[n, :, :, pl.ds(half * T, T)]
        src = a_buf.at[:, :, pl.ds(pl.multiple_of(to * DROWS + half * T, T), T)]
        k = n * 2 + half
        return remote(dst if incoming else src, dst, n_send.at[k], n_recv.at[k], (to, j))

    def near_send(half, *which):
        for n in which:
            copy = near_swap(n, half, False)
            copy.start()
            pending.append(copy)

    def near_wait(*which):
        for n in which:
            for half in range(2):
                near_swap(n, half, True).wait_recv()

    def heads_swap(r, incoming):
        there = (i - r) % NDP if incoming else (i + r) % NDP
        return remote(
            hbuf.at[i], hbuf.at[there if incoming else i], h_send.at[r], h_recv.at[r], ((i + r) % NDP, j)
        )

    up_copy.wait()
    pl.semaphore_wait(barrier, len(peers))
    stage("a", 0)
    for n in range(FAR):
        copy = swap(n, False)
        copy.start()
        pending.append(copy)
    for copy in small:
        copy.wait()

    row16 = lax.broadcasted_iota(jnp.int32, (16, T), 0)

    def fill(ref):
        out = jnp.zeros((16, T), F32)
        for h in range(HEADS):
            out = jnp.where(row16 == h, ref[h], out)
        return out

    rows[0] = jnp.zeros((16, T), F32)
    rows[0, 0:HEADS, :] = dtraw_ref[...]
    shifted = rows[0] + fill(bias_ref)
    dt = jnp.maximum(shifted, 0.0) + jnp.log1p(jnp.exp(-jnp.abs(shifted)))
    slope = 1.0 / (1.0 + jnp.exp(-shifted))
    decay = jnp.exp(fill(alog_ref))
    first = lax.broadcasted_iota(jnp.int32, (T, T), 0)
    second = lax.broadcasted_iota(jnp.int32, (T, T), 1)
    total = jnp.dot(
        dt * decay, jnp.where(first <= second, 1.0, 0.0), precision=HIGHEST, preferred_element_type=F32
    )
    rows[0] = total
    rows[1] = dt
    rows[2] = slope
    rows[3] = decay
    pack[...] = jnp.zeros((HALF, T), F32)
    pack[0:16, :] = total
    pack[16:32, :] = dt
    cols[...] = jnp.transpose(pack[...])

    in_copy.wait()
    bc_copy.wait()
    score[...] = dot_nt(bc_buf[:, NSTATE:], bc_buf[:, :NSTATE])
    score_t[...] = dot_nt(bc_buf[:, :NSTATE], bc_buf[:, NSTATE:])

    used = counts_ref[j]
    left = lax.broadcasted_iota(jnp.int32, (1, HALF), 1) < PW

    def per_lane(value, pair):
        return jnp.where(left, value(2 * pair), value(2 * pair + 1))

    def active(h):
        return jnp.where(h < used, 1.0, 0.0).astype(F32)

    def causal(rows_n, cols_n, row_start, col_start, lower):
        a = lax.broadcasted_iota(jnp.int32, (rows_n, cols_n), 0) + row_start
        b = lax.broadcasted_iota(jnp.int32, (rows_n, cols_n), 1) + col_start
        return a >= b if lower else a <= b

    def forward_pair(pair):
        lanes = slice(pair * HALF, (pair + 1) * HALF)
        values = x_buf[:, lanes]
        lane_skip = per_lane(lambda h: skip_ref[h], pair)
        lane_active = per_lane(active, pair)
        for block in range(2):
            end = (block + 1) * HALF
            here = slice(block * HALF, end)
            sides = []
            for h in (2 * pair, 2 * pair + 1):
                gap = rows[0, h : h + 1, 0:end] - cols[here, h : h + 1]
                gap = jnp.where(causal(HALF, end, block * HALF, 0, True), gap, -1e30)
                weights = jnp.exp(gap) * (score[here, 0:end] * rows[1, h : h + 1, 0:end])
                high, low = split(weights)
                sides.append(dot(high, values[0:end]) + dot(low, values[0:end]))
            scanned = jnp.where(left, sides[0], sides[1])
            yscan[here, lanes] = scanned
            out = (scanned + lane_skip * values[here].astype(F32)) * lane_active
            outs[FAR, here, lanes] = out.astype(BF16)

    forward_pair(0)
    forward_pair(1)
    stage("a", 1)
    forward_pair(2)
    forward_pair(3)
    forward_pair(4)
    ring_stage(0, 0)
    ring_stage(0, 1)
    stage("a", 2)
    for n in range(FAR):
        swap(n, True).wait_recv()
    ring_stage(1, 0)
    stage("a", 3)
    ring_stage(1, 1)
    stage("a", 4)
    stage("b", 0)
    ring_stage(2, 0)
    w_copy.wait()
    stage("a", 5)
    near_send(0, 0)
    near_send(1, 0)
    ring_stage(2, 1)

    depth = 1024

    def first_matmul(step, carry):
        at = pl.multiple_of(step * depth, depth)
        block = a_buf[:, :, pl.ds(at, depth)].reshape(T, depth)
        fgrad[...] += dot(block, w_buf[pl.ds(at, depth), :])
        return carry

    fgrad[...] = jnp.zeros((T, WIDTH), F32)
    lax.fori_loop(0, D // depth // 2, first_matmul, 0)
    stage("b", 1)
    lax.fori_loop(D // depth // 2, D // depth, first_matmul, 0)
    ring_stage(3, 0)
    near_send(0, 1, 2)

    dgt[...] = jnp.zeros((T, T), F32)

    def backward_pair(pair):
        lanes = slice(pair * HALF, (pair + 1) * HALF)
        values = x_buf[:, lanes]
        lane_skip = per_lane(lambda h: skip_ref[h], pair)
        grad = fgrad[:, lanes] * per_lane(active, pair)
        g_high, g_low = split(grad)
        both = jnp.concatenate([g_high, g_low], axis=1)
        for block in range(2):
            start = block * HALF
            here = slice(start, start + HALF)
            sides = []
            for side, h in enumerate((2 * pair, 2 * pair + 1)):
                gap = cols[here, h : h + 1] - rows[0, h : h + 1, start:]
                gap = jnp.where(causal(HALF, T - start, start, start, False), gap, -1e30)
                scale = jnp.exp(gap) * cols[here, 16 + h : 17 + h]
                high, low = split(scale * score_t[here, start:])
                two = dot(high, both[start:])
                sides.append(two[:, :HALF] + two[:, HALF:] + dot(low, g_high[start:]))
                mine = jnp.where(left if side == 0 else jnp.logical_not(left), values[here], jnp.zeros((), BF16))
                outer = dot_nt(jnp.concatenate([mine, mine], axis=1), both[start:])
                dgt[here, start:] += scale * outer
            scanned = jnp.where(left, sides[0], sides[1])
            g_here = grad[here]
            x_here = values[here].astype(F32)
            ig_ref[here, lanes] = (scanned + lane_skip * g_here).astype(BF16)
            xd[here, lanes] = x_here * scanned
            gy[here, lanes] = g_here * yscan[here, lanes]
            gx[here, lanes] = g_here * x_here

    backward_pair(0)
    backward_pair(1)
    stage("b", 2)
    backward_pair(2)
    backward_pair(3)
    ring_stage(3, 1)
    backward_pair(4)

    head_of = lax.broadcasted_iota(jnp.int32, (16, WIDTH), 1) // PW
    pick = jnp.where(head_of == lax.broadcasted_iota(jnp.int32, (16, WIDTH), 0), 1.0, 0.0)
    entry_sum = dot_nt(pick, xd[...], HIGHEST)
    exit_sum = dot_nt(pick, gy[...], HIGHEST)
    skip_sum = dot_nt(pick, gx[...], HIGHEST)
    rate_grad = jnp.dot(
        entry_sum - exit_sum,
        jnp.where(first >= second, 1.0, 0.0),
        precision=HIGHEST,
        preferred_element_type=F32,
    )
    dt_now, decay_now = rows[1], rows[3]
    raw_grad = (entry_sum / dt_now + rate_grad * decay_now) * rows[2]
    dtg_ref[...] = raw_grad[0:HEADS, :]
    alog_part = jnp.sum(rate_grad * dt_now * decay_now, axis=1, keepdims=True)
    skip_part = jnp.sum(skip_sum, axis=1, keepdims=True)
    bias_part = jnp.sum(raw_grad, axis=1, keepdims=True)
    lane16 = lax.broadcasted_iota(jnp.int32, (16, HALF), 1)
    hbuf[i] = jnp.where(
        lane16 == 0, alog_part, jnp.where(lane16 == 1, skip_part, jnp.where(lane16 == 2, bias_part, 0.0))
    )
    for r in range(1, NDP):
        copy = heads_swap(r, False)
        copy.start()
        pending.append(copy)
    near_send(1, 1, 2)

    stage("b", 3)
    low_high, low_low = split(dgt[...])
    gg_ref[:, :NSTATE] = (dot(low_high, bc_buf[:, NSTATE:]) + dot(low_low, bc_buf[:, NSTATE:])).astype(BF16)
    up_high, up_low = split(jnp.transpose(dgt[...]))
    gg_ref[:, NSTATE:] = (dot(up_high, bc_buf[:, :NSTATE]) + dot(up_low, bc_buf[:, :NSTATE])).astype(BF16)

    def second_matmul(dvs, low, high):
        for p in range(2):
            slots = [slot_of(p, du, dv) for dv in dvs for du in range(4)]
            here = slice(p * T, (p + 1) * T)
            left_side = jnp.concatenate([b_buf[s, low * 16 : high * 16, here] for s in slots], axis=0)
            right_side = jnp.concatenate(
                [
                    outs[low:high, pl.ds(pl.multiple_of(s * 16, 16), 16), :].reshape((high - low) * 16, WIDTH)
                    for s in slots
                ],
                axis=0,
            )
            wg_ref[here, :] += dot_tn(left_side, right_side)

    def chip_matmul():
        for p in range(2):
            here = slice(p * T, (p + 1) * T)
            mine = a_buf[:, :, pl.ds(pl.multiple_of(i * DROWS + p * T, T), T)].reshape(T, T)
            left_side = jnp.concatenate([mine, near[0, :, :, here].reshape(T, T)], axis=0)
            wg_ref[here, :] = dot_tn(left_side, outs[FAR : FAR + 2, :, :].reshape(2 * T, WIDTH))

    def near_matmul():
        for p in range(2):
            here = slice(p * T, (p + 1) * T)
            left_side = near[1:3, :, :, here].reshape(2 * T, T)
            wg_ref[here, :] += dot_tn(left_side, outs[FAR + 2 :, :, :].reshape(2 * T, WIDTH))

    near_wait(0)
    cross_waits((0, 1, 2, 3))
    chip_matmul()
    second_matmul((0,), 0, MOST)
    stage("b", 4)
    ring_stage(4, 0)
    ring_stage(4, 1)
    second_matmul((1,), 0, MOST)
    second_matmul((-1,), 0, MOST)
    cross_waits((4,))
    second_matmul((0, 1, -1), MOST, FAR)
    near_wait(1, 2)
    near_matmul()
    for r in range(1, NDP):
        heads_swap(r, True).wait_recv()
    tot = hbuf[0]
    for r in range(1, NDP):
        tot = tot + hbuf[r]
    eye = jnp.where(
        lax.broadcasted_iota(jnp.int32, (8, HALF), 0) == lax.broadcasted_iota(jnp.int32, (8, HALF), 1), 1.0, 0.0
    )
    hg_ref[...] = dot_nt(eye, tot, HIGHEST)[0:3, 0:HEADS]
    stage("b", 5)
    second_matmul((2,), 0, FAR)
    for copy in pending:
        copy.wait_send()


def publish(*refs):
    sems = refs[10]
    copies = [pltpu.make_async_copy(refs[n], refs[5 + n], sems.at[n]) for n in range(5)]
    for copy in copies:
        copy.start()
    for copy in copies:
        copy.wait()


def body(upstream, out_weight, inner, groups_bc, dt_raw, a_log, skip, dt_bias, head_counts):
    vmem = pl.BlockSpec(memory_space=pltpu.VMEM)
    hbm = pl.BlockSpec(memory_space=pl.ANY)
    dma = lambda n: pltpu.SemaphoreType.DMA((n,))
    shapes = (
        ((T, WIDTH), BF16),
        ((T, 2 * NSTATE), BF16),
        ((HEADS, T), F32),
        ((DROWS, WIDTH), F32),
        ((3, HEADS), F32),
    )
    results = pl.pallas_call(
        kernel,
        out_shape=tuple(pltpu.VMEM(*one) for one in shapes),
        in_specs=[hbm] * 9,
        out_specs=(vmem,) * 5,
        scratch_shapes=[
            pltpu.SMEM((HEADS,), F32),
            pltpu.SMEM((HEADS,), F32),
            pltpu.SMEM((HEADS,), F32),
            pltpu.SMEM((NT,), jnp.int32),
            pltpu.VMEM((HEADS, T), F32),
            pltpu.VMEM((NT, 16, D), BF16),
            pltpu.VMEM((NT, KB, DROWS), BF16),
            pltpu.VMEM((3, NT, 16, DROWS), BF16),
            pltpu.VMEM((NDP, T, WIDTH), BF16),
            pltpu.VMEM((D, WIDTH), BF16),
            pltpu.VMEM((T, WIDTH), BF16),
            pltpu.VMEM((T, 2 * NSTATE), BF16),
            pltpu.VMEM((4, 16, T), F32),
            pltpu.VMEM((T, HALF), F32),
            pltpu.VMEM((HALF, T), F32),
            pltpu.VMEM((T, T), F32),
            pltpu.VMEM((T, T), F32),
            pltpu.VMEM((T, WIDTH), F32),
            pltpu.VMEM((T, WIDTH), F32),
            pltpu.VMEM((T, T), F32),
            pltpu.VMEM((T, WIDTH), F32),
            pltpu.VMEM((T, WIDTH), F32),
            pltpu.VMEM((T, WIDTH), F32),
            pltpu.VMEM((NDP, 16, HALF), F32),
            dma(2 * NK), dma(2 * NK), dma(2 * NK), dma(2 * NK),
            dma(FAR), dma(FAR), dma(6), dma(6), dma(16), dma(16), dma(20), dma(20), dma(NDP), dma(NDP), dma(9),
        ],
        compiler_params=pltpu.CompilerParams(
            collective_id=0, has_side_effects=True, vmem_limit_bytes=56 * 1024 * 1024
        ),
    )(a_log, skip, dt_bias, head_counts, dt_raw, upstream, out_weight, inner, groups_bc)
    return pl.pallas_call(
        publish,
        out_shape=tuple(jax.ShapeDtypeStruct(*one) for one in shapes),
        in_specs=[vmem] * 5,
        out_specs=(hbm,) * 5,
        scratch_shapes=[dma(5)],
    )(*[pltpu.with_memory_space_constraint(one, pltpu.VMEM) for one in results])


def solution(mesh):
    return jax.shard_map(
        body,
        mesh=mesh,
        in_specs=(
            P(("dp", "tensor"), None),
            P(None, "tensor"),
            P("dp", "tensor"),
            P("dp", "tensor"),
            P("tensor", "dp"),
            P("tensor"),
            P("tensor"),
            P("tensor"),
            P(),
        ),
        out_specs=(
            P("dp", "tensor"),
            P("dp", "tensor"),
            P("tensor", "dp"),
            P("dp", "tensor"),
            P(None, "tensor"),
        ),
        check_vma=False,
    )
```

```python
import functools

import jax
import jax.numpy as jnp
from jax import lax
from jax.experimental import pallas as pl
from jax.experimental.pallas import tpu as pltpu
from jax.sharding import PartitionSpec as P

MESH = pl.DeviceIdType.MESH
HIGHEST = lax.Precision.HIGHEST
F32 = jnp.float32
BF16 = jnp.bfloat16

T = 256
HALF = 128
HEADS = 10
PW = 64
WIDTH = HEADS * PW
NSTATE = 256
D = 8192
NDP = 16
NT = 16
NZ = 8
DROWS = D // NDP
AH = D // 2
NT_DIMS = (((1,), (1,)), ((), ()))
TN_DIMS = (((0,), (0,)), ((), ()))

PLACES = [(dz, c) for dz in (2, 3, 5, 6) for c in (0, 1)] + [(1, 1), (7, 1), (4, 0), (4, 1)]
PLACES += [(0, 0), (0, 1), (1, 0), (7, 0)]
FAR = 12
MOST = 10
KB = FAR * 16

KINDS = {
    "M1+": ("u", 1, (0, 0), None),
    "M1-": ("u", -1, (0, 0), None),
    "M2+": ("u", 1, (-1, 0), 0),
    "M2-": ("u", -1, (1, 0), 1),
    "N1+": ("v", 1, (0, 0), None),
    "N1-": ("v", -1, (0, 0), None),
    "N2+": ("v", 1, (-1, 0), None),
    "N2-": ("v", -1, (-1, 0), None),
    "N3+": ("v", 1, (1, 0), None),
    "N3-": ("v", -1, (1, 0), None),
    "N4+": ("v", 1, (2, 0), 0),
    "N4-": ("v", -1, (2, 0), 0),
    "N5+": ("v", 1, (2, 0), 1),
    "N5-": ("v", -1, (2, 0), 1),
    "F1+": ("v", 1, (0, -1), 0),
    "F1-": ("v", -1, (0, 1), 1),
    "F2+": ("v", 1, (-1, -1), 0),
    "F2-": ("v", -1, (-1, 1), 1),
    "F3+": ("v", 1, (1, -1), 0),
    "F3-": ("v", -1, (1, 1), 1),
    "F4+": ("v", 1, (2, -1), 0),
    "F5-": ("v", -1, (2, 1), 1),
}
NAMES = list(KINDS)
NK = len(NAMES)


def remote(src, dst, send_sem, recv_sem, device):
    return pltpu.make_async_remote_copy(
        src_ref=src, dst_ref=dst, send_sem=send_sem, recv_sem=recv_sem, device_id=device, device_id_type=MESH
    )


def split(value):
    high = value.astype(BF16)
    return high, (value - high.astype(F32)).astype(BF16)


def dot(a, b):
    return jnp.dot(a, b, preferred_element_type=F32)


def dot_tn(a, b):
    return lax.dot_general(a, b, TN_DIMS, preferred_element_type=F32)


def dot_nt(a, b, precision=None):
    return lax.dot_general(a, b, NT_DIMS, precision=precision, preferred_element_type=F32)


def kernel(
    alog_hbm, skip_hbm, bias_hbm, counts_hbm, dtraw_hbm, up_ref, w_ref, inner_ref, groups_ref,
    ig_ref, gg_ref, dtg_ref, wg_ref, hg_ref,
    alog_ref, skip_ref, bias_ref, counts_ref, dtraw_ref, a_buf, b_buf, near, outs, w_buf, x_buf, bc_buf, rows, cols, pack, score, score_t, yscan, fgrad, dgt, xd, gy, gx, hbuf,
    a_send, a_recv, b_send, b_recv, s_send, s_recv, n_send, n_recv, z_send, z_recv, c_send, c_recv, h_send, h_recv, local,
):
    i = lax.axis_index("dp")
    j = lax.axis_index("tensor")
    z, core = i // 2, i % 2
    y, x = j // 4, j % 4
    pending = []

    barrier = pltpu.get_barrier_semaphore()
    peers = [(i, y * 4 + (x + s) % 4) for s in (1, -1)] + [(i, (y + s) % 4 * 4 + x) for s in (1, -1)]
    peers += [((i + r) % NDP, j) for r in range(1, NDP)]
    for peer in peers:
        pl.semaphore_signal(barrier, inc=1, device_id=peer, device_id_type=MESH)

    def fetch(n, src, dst):
        copy = pltpu.make_async_copy(src, dst, local.at[n])
        copy.start()
        return copy

    up_copy = fetch(0, up_ref, a_buf.at[j])
    small = [
        fetch(4, alog_hbm, alog_ref),
        fetch(5, skip_hbm, skip_ref),
        fetch(6, bias_hbm, bias_ref),
        fetch(7, counts_hbm, counts_ref),
        fetch(8, dtraw_hbm, dtraw_ref),
    ]
    bc_copy = fetch(2, groups_ref, bc_buf)
    in_copy = fetch(1, inner_ref, x_buf)
    w_copy = fetch(3, w_ref, w_buf)

    def slot_of(p, du, dv):
        if p == 0:
            return (y + dv) % 4 * 4 + (x + du) % 4
        return (y + du) % 4 * 4 + (x + dv) % 4

    def part(which, slot, p, q):
        if which == "a":
            size = AH if q is None else AH // 2
            return a_buf.at[slot, :, pl.ds(p * AH + (q or 0) * (AH // 2), size)]
        size = T if q is None else T // 2
        return b_buf.at[slot, :, pl.ds(p * T + (q or 0) * (T // 2), size)]

    sems = {"a": (a_send, a_recv), "b": (b_send, b_recv)}

    def message(which, p, name, incoming):
        axis, way, (du, dv), q = KINDS[name]
        if incoming:
            du, dv = (du - way, dv) if axis == "u" else (du, dv - way)
        region = part(which, slot_of(p, du, dv), p, q)
        device = (i, slot_of(p, way, 0) if axis == "u" else slot_of(p, 0, way))
        send, recv = sems[which]
        k = p * NK + NAMES.index(name)
        return remote(region, region, send.at[k], recv.at[k], device)

    def send(which, *names):
        for name in names:
            for p in range(2):
                copy = message(which, p, name, False)
                copy.start()
                pending.append(copy)

    def wait(which, *names):
        for name in names:
            for p in range(2):
                message(which, p, name, True).wait_recv()

    def stage(which, step):
        if step == 0:
            send(which, "M1+", "M1-", "N1+", "N1-")
        elif step == 1:
            wait(which, "M1+", "M1-")
            send(which, "M2+", "M2-", "N2+", "N2-", "N3+", "N3-")
        elif step == 2:
            wait(which, "M2+", "M2-")
            send(which, "N4+", "N4-", "N5+", "N5-")
            wait(which, "N1+", "N1-")
            send(which, "F1+", "F1-")
        elif step == 3:
            wait(which, "N2+", "N2-", "N3+", "N3-")
            send(which, "F2+", "F2-", "F3+", "F3-")
        elif step == 4:
            wait(which, "N4+", "N4-", "N5+", "N5-")
            send(which, "F4+", "F5-")
        else:
            wait(which, "F1+", "F1-", "F2+", "F2-", "F3+", "F3-", "F4+", "F5-")

    def place(dz, other):
        return PLACES.index((dz % NZ, other))

    def half_block(at, q):
        return outs.at[at, pl.ds(q * HALF, HALF), :]

    def ring(k, way, q, incoming):
        here, there = half_block(place(-way * k, 0), q), half_block(place(-way * (k + 1), 0), q)
        n = (k * 2 + q) * 2 + (way + 1) // 2
        return remote(
            there if incoming else here, there, z_send.at[n], z_recv.at[n], ((z + way) % NZ * 2 + core, j)
        )

    def cross(k, way, q, incoming):
        here, there = half_block(place(-way * k, 0), q), half_block(place(-way * k, 1), q)
        n = (k * 2 + q) * 2 + (way + 1) // 2
        return remote(there if incoming else here, there, c_send.at[n], c_recv.at[n], (z * 2 + 1 - core, j))

    def goes(k, way, q):
        return k < 3 or q == (0 if way == 1 else 1)

    def ring_stage(step, q):
        for way in (1, -1):
            if step > 0:
                if not goes(step - 1, way, q):
                    continue
                ring(step - 1, way, q, True).wait_recv()
            copies = []
            if step < 4 and goes(step, way, q):
                copies.append(ring(step, way, q, False))
            if step > 0 or way == 1:
                copies.append(cross(step, way, q, False))
            for copy in copies:
                copy.start()
                pending.append(copy)

    def cross_waits(hops):
        for k in hops:
            for q in range(2):
                for way in (1, -1) if k > 0 else (1,):
                    if goes(k - 1, way, q):
                        cross(k, way, q, True).wait_recv()

    def columns(dp):
        return pl.ds(pl.multiple_of(dp * DROWS, DROWS), DROWS)

    def at_place(dz, other):
        return (z + dz) % NZ * 2 + (core + other) % 2

    def swap(n, incoming):
        dz, other = PLACES[n]
        to = at_place(-dz, other)
        dst = b_buf.at[j, pl.ds(n * 16, 16), :]
        src = dst if incoming else a_buf.at[j, :, columns(to)]
        return remote(src, dst, s_send.at[n], s_recv.at[n], (to, j))

    def near_swap(n, half, incoming):
        dz, other = PLACES[FAR + 1 + n]
        to = at_place(-dz, other)
        dst = near.at[n, :, :, pl.ds(half * T, T)]
        src = a_buf.at[:, :, pl.ds(pl.multiple_of(to * DROWS + half * T, T), T)]
        k = n * 2 + half
        return remote(dst if incoming else src, dst, n_send.at[k], n_recv.at[k], (to, j))

    def near_send(half, *which):
        for n in which:
            copy = near_swap(n, half, False)
            copy.start()
            pending.append(copy)

    def near_wait(*which):
        for n in which:
            for half in range(2):
                near_swap(n, half, True).wait_recv()

    def heads_swap(r, incoming):
        there = (i - r) % NDP if incoming else (i + r) % NDP
        return remote(
            hbuf.at[i], hbuf.at[there if incoming else i], h_send.at[r], h_recv.at[r], ((i + r) % NDP, j)
        )

    for copy in small:
        copy.wait()
    row16 = lax.broadcasted_iota(jnp.int32, (16, T), 0)

    def fill(ref):
        out = jnp.zeros((16, T), F32)
        for h in range(HEADS):
            out = jnp.where(row16 == h, ref[h], out)
        return out

    rows[0] = jnp.zeros((16, T), F32)
    rows[0, 0:HEADS, :] = dtraw_ref[...]
    shifted = rows[0] + fill(bias_ref)
    dt = jnp.maximum(shifted, 0.0) + jnp.log1p(jnp.exp(-jnp.abs(shifted)))
    slope = 1.0 / (1.0 + jnp.exp(-shifted))
    decay = jnp.exp(fill(alog_ref))
    first = lax.broadcasted_iota(jnp.int32, (T, T), 0)
    second = lax.broadcasted_iota(jnp.int32, (T, T), 1)
    total = jnp.dot(
        dt * decay, jnp.where(first <= second, 1.0, 0.0), precision=HIGHEST, preferred_element_type=F32
    )
    rows[0] = total
    rows[1] = dt
    rows[2] = slope
    rows[3] = decay
    pack[...] = jnp.zeros((HALF, T), F32)
    pack[0:16, :] = total
    pack[16:32, :] = dt
    cols[...] = jnp.transpose(pack[...])

    up_copy.wait()
    pl.semaphore_wait(barrier, len(peers))
    stage("a", 0)

    def swap_send(*which):
        for n in which:
            copy = swap(n, False)
            copy.start()
            pending.append(copy)

    swap_send(*range(0, FAR, 2))

    in_copy.wait()
    bc_copy.wait()
    score[...] = dot_nt(bc_buf[:, NSTATE:], bc_buf[:, :NSTATE])
    score_t[...] = dot_nt(bc_buf[:, :NSTATE], bc_buf[:, NSTATE:])

    used = counts_ref[j]
    left = lax.broadcasted_iota(jnp.int32, (1, HALF), 1) < PW

    def per_lane(value, pair):
        return jnp.where(left, value(2 * pair), value(2 * pair + 1))

    def active(h):
        return jnp.where(h < used, 1.0, 0.0).astype(F32)

    def causal(rows_n, cols_n, row_start, col_start, lower):
        a = lax.broadcasted_iota(jnp.int32, (rows_n, cols_n), 0) + row_start
        b = lax.broadcasted_iota(jnp.int32, (rows_n, cols_n), 1) + col_start
        return a >= b if lower else a <= b

    def forward_pair(pair, block):
        lanes = slice(pair * HALF, (pair + 1) * HALF)
        values = x_buf[:, lanes]
        lane_skip = per_lane(lambda h: skip_ref[h], pair)
        lane_active = per_lane(active, pair)
        end = (block + 1) * HALF
        here = slice(block * HALF, end)
        sides = []
        for h in (2 * pair, 2 * pair + 1):
            gap = rows[0, h : h + 1, 0:end] - cols[here, h : h + 1]
            gap = jnp.where(causal(HALF, end, block * HALF, 0, True), gap, -1e30)
            weights = jnp.exp(gap) * (score[here, 0:end] * rows[1, h : h + 1, 0:end])
            high, low = split(weights)
            sides.append(dot(high, values[0:end]) + dot(low, values[0:end]))
        scanned = jnp.where(left, sides[0], sides[1])
        yscan[here, lanes] = scanned
        out = (scanned + lane_skip * values[here].astype(F32)) * lane_active
        outs[FAR, here, lanes] = out.astype(BF16)

    for pair in range(5):
        forward_pair(pair, 0)
    ring_stage(0, 0)
    forward_pair(0, 1)
    stage("a", 1)
    for pair in range(1, 5):
        forward_pair(pair, 1)
    ring_stage(0, 1)
    swap_send(*range(1, FAR, 2))
    stage("a", 2)
    ring_stage(1, 0)
    stage("a", 3)
    ring_stage(1, 1)
    stage("a", 4)
    for n in range(FAR):
        swap(n, True).wait_recv()
    stage("b", 0)
    ring_stage(2, 0)
    w_copy.wait()
    stage("a", 5)
    near_send(0, 0)
    near_send(1, 0)
    ring_stage(2, 1)

    depth = 4096

    def first_matmul(step, carry):
        at = pl.multiple_of(step * depth, depth)
        block = a_buf[:, :, pl.ds(at, depth)].reshape(T, depth)
        fgrad[...] += dot(block, w_buf[pl.ds(at, depth), :])
        return carry

    fgrad[...] = jnp.zeros((T, WIDTH), F32)
    lax.fori_loop(0, D // depth // 2, first_matmul, 0)
    stage("b", 1)
    lax.fori_loop(D // depth // 2, D // depth, first_matmul, 0)
    ring_stage(3, 0)
    near_send(0, 1, 2)

    dgt[...] = jnp.zeros((T, T), F32)

    def backward_pair(pair):
        lanes = slice(pair * HALF, (pair + 1) * HALF)
        values = x_buf[:, lanes]
        lane_skip = per_lane(lambda h: skip_ref[h], pair)
        grad = fgrad[:, lanes] * per_lane(active, pair)
        g_high, g_low = split(grad)
        both = jnp.concatenate([g_high, g_low], axis=1)
        for block in range(2):
            start = block * HALF
            here = slice(start, start + HALF)
            sides = []
            for side, h in enumerate((2 * pair, 2 * pair + 1)):
                gap = cols[here, h : h + 1] - rows[0, h : h + 1, start:]
                gap = jnp.where(causal(HALF, T - start, start, start, False), gap, -1e30)
                scale = jnp.exp(gap) * cols[here, 16 + h : 17 + h]
                high, low = split(scale * score_t[here, start:])
                two = dot(high, both[start:])
                sides.append(two[:, :HALF] + two[:, HALF:] + dot(low, g_high[start:]))
                mine = jnp.where(left if side == 0 else jnp.logical_not(left), values[here], jnp.zeros((), BF16))
                outer = dot_nt(jnp.concatenate([mine, mine], axis=1), both[start:])
                dgt[here, start:] += scale * outer
            scanned = jnp.where(left, sides[0], sides[1])
            g_here = grad[here]
            x_here = values[here].astype(F32)
            ig_ref[here, lanes] = (scanned + lane_skip * g_here).astype(BF16)
            xd[here, lanes] = x_here * scanned
            gy[here, lanes] = g_here * yscan[here, lanes]
            gx[here, lanes] = g_here * x_here

    backward_pair(0)
    backward_pair(1)
    stage("b", 2)
    backward_pair(2)
    backward_pair(3)
    ring_stage(3, 1)
    backward_pair(4)

    head_of = lax.broadcasted_iota(jnp.int32, (16, WIDTH), 1) // PW
    pick = jnp.where(head_of == lax.broadcasted_iota(jnp.int32, (16, WIDTH), 0), 1.0, 0.0)
    entry_sum = dot_nt(pick, xd[...], HIGHEST)
    exit_sum = dot_nt(pick, gy[...], HIGHEST)
    skip_sum = dot_nt(pick, gx[...], HIGHEST)
    rate_grad = jnp.dot(
        entry_sum - exit_sum,
        jnp.where(first >= second, 1.0, 0.0),
        precision=HIGHEST,
        preferred_element_type=F32,
    )
    dt_now, decay_now = rows[1], rows[3]
    raw_grad = (entry_sum / dt_now + rate_grad * decay_now) * rows[2]
    dtg_ref[...] = raw_grad[0:HEADS, :]
    alog_part = jnp.sum(rate_grad * dt_now * decay_now, axis=1, keepdims=True)
    skip_part = jnp.sum(skip_sum, axis=1, keepdims=True)
    bias_part = jnp.sum(raw_grad, axis=1, keepdims=True)
    lane16 = lax.broadcasted_iota(jnp.int32, (16, HALF), 1)
    hbuf[i] = jnp.where(
        lane16 == 0, alog_part, jnp.where(lane16 == 1, skip_part, jnp.where(lane16 == 2, bias_part, 0.0))
    )
    for r in range(1, NDP):
        copy = heads_swap(r, False)
        copy.start()
        pending.append(copy)
    near_send(1, 1, 2)

    low_high, low_low = split(dgt[...])
    gg_ref[:, :NSTATE] = (dot(low_high, bc_buf[:, NSTATE:]) + dot(low_low, bc_buf[:, NSTATE:])).astype(BF16)
    up_high, up_low = split(jnp.transpose(dgt[...]))
    gg_ref[:, NSTATE:] = (dot(up_high, bc_buf[:, :NSTATE]) + dot(up_low, bc_buf[:, :NSTATE])).astype(BF16)

    def second_matmul(dvs, low, high):
        for p in range(2):
            slots = [slot_of(p, du, dv) for dv in dvs for du in range(4)]
            here = slice(p * T, (p + 1) * T)
            left_side = jnp.concatenate([b_buf[s, low * 16 : high * 16, here] for s in slots], axis=0)
            right_side = jnp.concatenate(
                [
                    outs[low:high, pl.ds(pl.multiple_of(s * 16, 16), 16), :].reshape((high - low) * 16, WIDTH)
                    for s in slots
                ],
                axis=0,
            )
            wg_ref[here, :] += dot_tn(left_side, right_side)

    def chip_matmul():
        for p in range(2):
            here = slice(p * T, (p + 1) * T)
            mine = a_buf[:, :, pl.ds(pl.multiple_of(i * DROWS + p * T, T), T)].reshape(T, T)
            left_side = jnp.concatenate([mine, near[0, :, :, here].reshape(T, T)], axis=0)
            wg_ref[here, :] = dot_tn(left_side, outs[FAR : FAR + 2, :, :].reshape(2 * T, WIDTH))

    def near_matmul():
        for p in range(2):
            here = slice(p * T, (p + 1) * T)
            left_side = near[1:3, :, :, here].reshape(2 * T, T)
            wg_ref[here, :] += dot_tn(left_side, outs[FAR + 2 :, :, :].reshape(2 * T, WIDTH))

    near_wait(0)
    cross_waits((0, 1))
    chip_matmul()
    stage("b", 3)
    cross_waits((2, 3))
    second_matmul((0,), 0, MOST)
    stage("b", 4)
    ring_stage(4, 0)
    ring_stage(4, 1)
    second_matmul((1,), 0, MOST)
    second_matmul((-1,), 0, MOST)
    cross_waits((4,))
    second_matmul((0, 1, -1), MOST, FAR)
    near_wait(1, 2)
    near_matmul()
    for r in range(1, NDP):
        heads_swap(r, True).wait_recv()
    tot = hbuf[0]
    for r in range(1, NDP):
        tot = tot + hbuf[r]
    eye = jnp.where(
        lax.broadcasted_iota(jnp.int32, (8, HALF), 0) == lax.broadcasted_iota(jnp.int32, (8, HALF), 1), 1.0, 0.0
    )
    hg_ref[...] = dot_nt(eye, tot, HIGHEST)[0:3, 0:HEADS]
    last = 20
    for copy in pending[:-last]:
        copy.wait_send()
    stage("b", 5)
    second_matmul((2,), 0, FAR)
    for copy in pending[-last:]:
        copy.wait_send()


def publish(*refs):
    sems = refs[10]
    copies = [pltpu.make_async_copy(refs[n], refs[5 + n], sems.at[n]) for n in range(5)]
    for copy in copies:
        copy.start()
    for copy in copies:
        copy.wait()


def body(upstream, out_weight, inner, groups_bc, dt_raw, a_log, skip, dt_bias, head_counts):
    vmem = pl.BlockSpec(memory_space=pltpu.VMEM)
    hbm = pl.BlockSpec(memory_space=pl.ANY)
    dma = lambda n: pltpu.SemaphoreType.DMA((n,))
    shapes = (
        ((T, WIDTH), BF16),
        ((T, 2 * NSTATE), BF16),
        ((HEADS, T), F32),
        ((DROWS, WIDTH), F32),
        ((3, HEADS), F32),
    )
    results = pl.pallas_call(
        kernel,
        out_shape=tuple(pltpu.VMEM(*one) for one in shapes),
        in_specs=[hbm] * 9,
        out_specs=(vmem,) * 5,
        scratch_shapes=[
            pltpu.SMEM((HEADS,), F32),
            pltpu.SMEM((HEADS,), F32),
            pltpu.SMEM((HEADS,), F32),
            pltpu.SMEM((NT,), jnp.int32),
            pltpu.VMEM((HEADS, T), F32),
            pltpu.VMEM((NT, 16, D), BF16),
            pltpu.VMEM((NT, KB, DROWS), BF16),
            pltpu.VMEM((3, NT, 16, DROWS), BF16),
            pltpu.VMEM((NDP, T, WIDTH), BF16),
            pltpu.VMEM((D, WIDTH), BF16),
            pltpu.VMEM((T, WIDTH), BF16),
            pltpu.VMEM((T, 2 * NSTATE), BF16),
            pltpu.VMEM((4, 16, T), F32),
            pltpu.VMEM((T, HALF), F32),
            pltpu.VMEM((HALF, T), F32),
            pltpu.VMEM((T, T), F32),
            pltpu.VMEM((T, T), F32),
            pltpu.VMEM((T, WIDTH), F32),
            pltpu.VMEM((T, WIDTH), F32),
            pltpu.VMEM((T, T), F32),
            pltpu.VMEM((T, WIDTH), F32),
            pltpu.VMEM((T, WIDTH), F32),
            pltpu.VMEM((T, WIDTH), F32),
            pltpu.VMEM((NDP, 16, HALF), F32),
            dma(2 * NK), dma(2 * NK), dma(2 * NK), dma(2 * NK),
            dma(FAR), dma(FAR), dma(6), dma(6), dma(16), dma(16), dma(20), dma(20), dma(NDP), dma(NDP), dma(9),
        ],
        compiler_params=pltpu.CompilerParams(
            collective_id=0, has_side_effects=True, vmem_limit_bytes=56 * 1024 * 1024
        ),
    )(a_log, skip, dt_bias, head_counts, dt_raw, upstream, out_weight, inner, groups_bc)
    return pl.pallas_call(
        publish,
        out_shape=tuple(jax.ShapeDtypeStruct(*one) for one in shapes),
        in_specs=[vmem] * 5,
        out_specs=(hbm,) * 5,
        scratch_shapes=[dma(5)],
    )(*[pltpu.with_memory_space_constraint(one, pltpu.VMEM) for one in results])


def solution(mesh):
    return jax.shard_map(
        body,
        mesh=mesh,
        in_specs=(
            P(("dp", "tensor"), None),
            P(None, "tensor"),
            P("dp", "tensor"),
            P("dp", "tensor"),
            P("tensor", "dp"),
            P("tensor"),
            P("tensor"),
            P("tensor"),
            P(),
        ),
        out_specs=(
            P("dp", "tensor"),
            P("dp", "tensor"),
            P("tensor", "dp"),
            P("dp", "tensor"),
            P(None, "tensor"),
        ),
        check_vma=False,
    )
```

```python
import functools

import jax
import jax.numpy as jnp
from jax import lax
from jax.experimental import pallas as pl
from jax.experimental.pallas import tpu as pltpu
from jax.sharding import PartitionSpec as P

MESH = pl.DeviceIdType.MESH
HIGHEST = lax.Precision.HIGHEST
F32 = jnp.float32
BF16 = jnp.bfloat16

T = 256
HALF = 128
HEADS = 10
PW = 64
WIDTH = HEADS * PW
NSTATE = 256
D = 8192
NDP = 16
NT = 16
NZ = 8
DROWS = D // NDP
AH = D // 2
NT_DIMS = (((1,), (1,)), ((), ()))
TN_DIMS = (((0,), (0,)), ((), ()))

PLACES = [(dz, c) for dz in (2, 3, 5, 6) for c in (0, 1)] + [(1, 1), (7, 1), (4, 0), (4, 1)]
PLACES += [(0, 0), (0, 1), (1, 0), (7, 0)]
FAR = 12
MOST = 10
KB = FAR * 16

KINDS = {
    "M1+": ("u", 1, (0, 0), None),
    "M1-": ("u", -1, (0, 0), None),
    "M2+": ("u", 1, (-1, 0), 0),
    "M2-": ("u", -1, (1, 0), 1),
    "N1+": ("v", 1, (0, 0), None),
    "N1-": ("v", -1, (0, 0), None),
    "N2+": ("v", 1, (-1, 0), None),
    "N2-": ("v", -1, (-1, 0), None),
    "N3+": ("v", 1, (1, 0), None),
    "N3-": ("v", -1, (1, 0), None),
    "N4+": ("v", 1, (2, 0), 0),
    "N4-": ("v", -1, (2, 0), 0),
    "N5+": ("v", 1, (2, 0), 1),
    "N5-": ("v", -1, (2, 0), 1),
    "F1+": ("v", 1, (0, -1), 0),
    "F1-": ("v", -1, (0, 1), 1),
    "F2+": ("v", 1, (-1, -1), 0),
    "F2-": ("v", -1, (-1, 1), 1),
    "F3+": ("v", 1, (1, -1), 0),
    "F3-": ("v", -1, (1, 1), 1),
    "F4+": ("v", 1, (2, -1), 0),
    "F5-": ("v", -1, (2, 1), 1),
}
NAMES = list(KINDS)
NK = len(NAMES)


def remote(src, dst, send_sem, recv_sem, device):
    return pltpu.make_async_remote_copy(
        src_ref=src, dst_ref=dst, send_sem=send_sem, recv_sem=recv_sem, device_id=device, device_id_type=MESH
    )


def split(value):
    high = value.astype(BF16)
    return high, (value - high.astype(F32)).astype(BF16)


def dot(a, b):
    return jnp.dot(a, b, preferred_element_type=F32)


def dot_tn(a, b):
    return lax.dot_general(a, b, TN_DIMS, preferred_element_type=F32)


def dot_nt(a, b, precision=None):
    return lax.dot_general(a, b, NT_DIMS, precision=precision, preferred_element_type=F32)


def kernel(
    alog_hbm, skip_hbm, bias_hbm, counts_hbm, dtraw_hbm, up_ref, w_ref, inner_ref, groups_ref,
    ig_ref, gg_ref, dtg_ref, wg_ref, hg_ref,
    alog_ref, skip_ref, bias_ref, counts_ref, dtraw_ref, a_buf, b_buf, near, outs, w_buf, x_buf, bc_buf, rows, cols, pack, score, score_t, yscan, fgrad, dgt, xd, gy, gx, hbuf,
    a_send, a_recv, b_send, b_recv, s_send, s_recv, n_send, n_recv, z_send, z_recv, c_send, c_recv, h_send, h_recv, local,
):
    i = lax.axis_index("dp")
    j = lax.axis_index("tensor")
    z, core = i // 2, i % 2
    y, x = j // 4, j % 4
    pending = []

    barrier = pltpu.get_barrier_semaphore()
    peers = [(i, y * 4 + (x + s) % 4) for s in (1, -1)] + [(i, (y + s) % 4 * 4 + x) for s in (1, -1)]
    peers += [((i + r) % NDP, j) for r in range(1, NDP)]
    for peer in peers:
        pl.semaphore_signal(barrier, inc=1, device_id=peer, device_id_type=MESH)

    def fetch(n, src, dst):
        copy = pltpu.make_async_copy(src, dst, local.at[n])
        copy.start()
        return copy

    up_copy = fetch(0, up_ref, a_buf.at[j])
    small = [
        fetch(4, alog_hbm, alog_ref),
        fetch(5, skip_hbm, skip_ref),
        fetch(6, bias_hbm, bias_ref),
        fetch(7, counts_hbm, counts_ref),
        fetch(8, dtraw_hbm, dtraw_ref),
    ]
    bc_copy = fetch(2, groups_ref, bc_buf)
    in_copy = fetch(1, inner_ref, x_buf)
    w_copy = fetch(3, w_ref, w_buf)

    def slot_of(p, du, dv):
        if p == 0:
            return (y + dv) % 4 * 4 + (x + du) % 4
        return (y + du) % 4 * 4 + (x + dv) % 4

    def part(which, slot, p, q):
        if which == "a":
            size = AH if q is None else AH // 2
            return a_buf.at[slot, :, pl.ds(p * AH + (q or 0) * (AH // 2), size)]
        size = T if q is None else T // 2
        return b_buf.at[slot, :, pl.ds(p * T + (q or 0) * (T // 2), size)]

    sems = {"a": (a_send, a_recv), "b": (b_send, b_recv)}

    def message(which, p, name, incoming):
        axis, way, (du, dv), q = KINDS[name]
        if incoming:
            du, dv = (du - way, dv) if axis == "u" else (du, dv - way)
        region = part(which, slot_of(p, du, dv), p, q)
        device = (i, slot_of(p, way, 0) if axis == "u" else slot_of(p, 0, way))
        send, recv = sems[which]
        k = p * NK + NAMES.index(name)
        return remote(region, region, send.at[k], recv.at[k], device)

    def send(which, *names):
        for name in names:
            for p in range(2):
                copy = message(which, p, name, False)
                copy.start()
                pending.append(copy)

    def wait(which, *names):
        for name in names:
            for p in range(2):
                message(which, p, name, True).wait_recv()

    def stage(which, step):
        if step == 0:
            send(which, "M1+", "M1-", "N1+", "N1-")
        elif step == 1:
            wait(which, "M1+", "M1-")
            send(which, "M2+", "M2-", "N2+", "N2-", "N3+", "N3-")
        elif step == 2:
            wait(which, "M2+", "M2-")
            send(which, "N4+", "N4-", "N5+", "N5-")
            wait(which, "N1+", "N1-")
            send(which, "F1+", "F1-")
        elif step == 3:
            wait(which, "N2+", "N2-", "N3+", "N3-")
            send(which, "F2+", "F2-", "F3+", "F3-")
        elif step == 4:
            wait(which, "N4+", "N4-", "N5+", "N5-")
            send(which, "F4+", "F5-")
        else:
            wait(which, "F1+", "F1-", "F2+", "F2-", "F3+", "F3-", "F4+", "F5-")

    def place(dz, other):
        return PLACES.index((dz % NZ, other))

    def half_block(at, q):
        return outs.at[at, pl.ds(q * HALF, HALF), :]

    def ring(k, way, q, incoming):
        here, there = half_block(place(-way * k, 0), q), half_block(place(-way * (k + 1), 0), q)
        n = (k * 2 + q) * 2 + (way + 1) // 2
        return remote(
            there if incoming else here, there, z_send.at[n], z_recv.at[n], ((z + way) % NZ * 2 + core, j)
        )

    def cross(k, way, q, incoming):
        here, there = half_block(place(-way * k, 0), q), half_block(place(-way * k, 1), q)
        n = (k * 2 + q) * 2 + (way + 1) // 2
        return remote(there if incoming else here, there, c_send.at[n], c_recv.at[n], (z * 2 + 1 - core, j))

    def goes(k, way, q):
        return k < 3 or q == (0 if way == 1 else 1)

    def ring_stage(step, q):
        for way in (1, -1):
            if step > 0:
                if not goes(step - 1, way, q):
                    continue
                ring(step - 1, way, q, True).wait_recv()
            copies = []
            if step < 4 and goes(step, way, q):
                copies.append(ring(step, way, q, False))
            if step > 0 or way == 1:
                copies.append(cross(step, way, q, False))
            for copy in copies:
                copy.start()
                pending.append(copy)

    def cross_waits(hops):
        for k in hops:
            for q in range(2):
                for way in (1, -1) if k > 0 else (1,):
                    if goes(k - 1, way, q):
                        cross(k, way, q, True).wait_recv()

    def columns(dp):
        return pl.ds(pl.multiple_of(dp * DROWS, DROWS), DROWS)

    def at_place(dz, other):
        return (z + dz) % NZ * 2 + (core + other) % 2

    def swap(n, incoming):
        dz, other = PLACES[n]
        to = at_place(-dz, other)
        dst = b_buf.at[j, pl.ds(n * 16, 16), :]
        src = dst if incoming else a_buf.at[j, :, columns(to)]
        return remote(src, dst, s_send.at[n], s_recv.at[n], (to, j))

    def near_swap(n, half, incoming):
        dz, other = PLACES[FAR + 1 + n]
        to = at_place(-dz, other)
        dst = near.at[n, :, :, pl.ds(half * T, T)]
        src = a_buf.at[:, :, pl.ds(pl.multiple_of(to * DROWS + half * T, T), T)]
        k = n * 2 + half
        return remote(dst if incoming else src, dst, n_send.at[k], n_recv.at[k], (to, j))

    def near_send(half, *which):
        for n in which:
            copy = near_swap(n, half, False)
            copy.start()
            pending.append(copy)

    def near_wait(halves, *which):
        for n in which:
            for half in halves:
                near_swap(n, half, True).wait_recv()

    def heads_swap(r, incoming):
        there = (i - r) % NDP if incoming else (i + r) % NDP
        return remote(
            hbuf.at[i], hbuf.at[there if incoming else i], h_send.at[r], h_recv.at[r], ((i + r) % NDP, j)
        )

    for copy in small:
        copy.wait()
    row16 = lax.broadcasted_iota(jnp.int32, (16, T), 0)

    def fill(ref):
        out = jnp.zeros((16, T), F32)
        for h in range(HEADS):
            out = jnp.where(row16 == h, ref[h], out)
        return out

    rows[0] = jnp.zeros((16, T), F32)
    rows[0, 0:HEADS, :] = dtraw_ref[...]
    shifted = rows[0] + fill(bias_ref)
    dt = jnp.maximum(shifted, 0.0) + jnp.log1p(jnp.exp(-jnp.abs(shifted)))
    slope = 1.0 / (1.0 + jnp.exp(-shifted))
    decay = jnp.exp(fill(alog_ref))
    first = lax.broadcasted_iota(jnp.int32, (T, T), 0)
    second = lax.broadcasted_iota(jnp.int32, (T, T), 1)
    total = jnp.dot(
        dt * decay, jnp.where(first <= second, 1.0, 0.0), precision=HIGHEST, preferred_element_type=F32
    )
    rows[0] = total
    rows[1] = dt
    rows[2] = slope
    rows[3] = decay
    pack[...] = jnp.zeros((HALF, T), F32)
    pack[0:16, :] = total
    pack[16:32, :] = dt
    cols[...] = jnp.transpose(pack[...])

    up_copy.wait()
    pl.semaphore_wait(barrier, len(peers))
    stage("a", 0)

    def swap_send(*which):
        for n in which:
            copy = swap(n, False)
            copy.start()
            pending.append(copy)

    swap_send(*range(0, FAR, 2))

    in_copy.wait()
    bc_copy.wait()
    score[...] = dot_nt(bc_buf[:, NSTATE:], bc_buf[:, :NSTATE])
    score_t[...] = dot_nt(bc_buf[:, :NSTATE], bc_buf[:, NSTATE:])

    used = counts_ref[j]
    left = lax.broadcasted_iota(jnp.int32, (1, HALF), 1) < PW

    def per_lane(value, pair):
        return jnp.where(left, value(2 * pair), value(2 * pair + 1))

    def active(h):
        return jnp.where(h < used, 1.0, 0.0).astype(F32)

    def causal(rows_n, cols_n, row_start, col_start, lower):
        a = lax.broadcasted_iota(jnp.int32, (rows_n, cols_n), 0) + row_start
        b = lax.broadcasted_iota(jnp.int32, (rows_n, cols_n), 1) + col_start
        return a >= b if lower else a <= b

    def forward_pair(pair, block):
        lanes = slice(pair * HALF, (pair + 1) * HALF)
        values = x_buf[:, lanes]
        lane_skip = per_lane(lambda h: skip_ref[h], pair)
        lane_active = per_lane(active, pair)
        end = (block + 1) * HALF
        here = slice(block * HALF, end)
        sides = []
        for h in (2 * pair, 2 * pair + 1):
            gap = rows[0, h : h + 1, 0:end] - cols[here, h : h + 1]
            gap = jnp.where(causal(HALF, end, block * HALF, 0, True), gap, -1e30)
            weights = jnp.exp(gap) * (score[here, 0:end] * rows[1, h : h + 1, 0:end])
            high, low = split(weights)
            sides.append(dot(high, values[0:end]) + dot(low, values[0:end]))
        scanned = jnp.where(left, sides[0], sides[1])
        yscan[here, lanes] = scanned
        out = (scanned + lane_skip * values[here].astype(F32)) * lane_active
        outs[FAR, here, lanes] = out.astype(BF16)

    for pair in range(5):
        forward_pair(pair, 0)
    ring_stage(0, 0)
    forward_pair(0, 1)
    stage("a", 1)
    for pair in range(1, 5):
        forward_pair(pair, 1)
    ring_stage(0, 1)
    swap_send(*range(1, FAR, 2))
    stage("a", 2)
    ring_stage(1, 0)
    stage("a", 3)
    ring_stage(1, 1)
    stage("a", 4)
    for n in range(FAR):
        swap(n, True).wait_recv()
    stage("b", 0)
    ring_stage(2, 0)
    w_copy.wait()
    stage("a", 5)
    near_send(0, 0)
    near_send(1, 0)
    ring_stage(2, 1)

    depth = 4096

    def first_matmul(step, carry):
        at = pl.multiple_of(step * depth, depth)
        block = a_buf[:, :, pl.ds(at, depth)].reshape(T, depth)
        fgrad[...] += dot(block, w_buf[pl.ds(at, depth), :])
        return carry

    fgrad[...] = jnp.zeros((T, WIDTH), F32)
    lax.fori_loop(0, D // depth // 2, first_matmul, 0)
    stage("b", 1)
    lax.fori_loop(D // depth // 2, D // depth, first_matmul, 0)
    ring_stage(3, 0)
    near_send(0, 1, 2)

    dgt[...] = jnp.zeros((T, T), F32)

    def backward_pair(pair):
        lanes = slice(pair * HALF, (pair + 1) * HALF)
        values = x_buf[:, lanes]
        lane_skip = per_lane(lambda h: skip_ref[h], pair)
        grad = fgrad[:, lanes] * per_lane(active, pair)
        g_high, g_low = split(grad)
        both = jnp.concatenate([g_high, g_low], axis=1)
        for block in range(2):
            start = block * HALF
            here = slice(start, start + HALF)
            sides = []
            for side, h in enumerate((2 * pair, 2 * pair + 1)):
                gap = cols[here, h : h + 1] - rows[0, h : h + 1, start:]
                gap = jnp.where(causal(HALF, T - start, start, start, False), gap, -1e30)
                scale = jnp.exp(gap) * cols[here, 16 + h : 17 + h]
                high, low = split(scale * score_t[here, start:])
                two = dot(high, both[start:])
                sides.append(two[:, :HALF] + two[:, HALF:] + dot(low, g_high[start:]))
                mine = jnp.where(left if side == 0 else jnp.logical_not(left), values[here], jnp.zeros((), BF16))
                outer = dot_nt(jnp.concatenate([mine, mine], axis=1), both[start:])
                dgt[here, start:] += scale * outer
            scanned = jnp.where(left, sides[0], sides[1])
            g_here = grad[here]
            x_here = values[here].astype(F32)
            ig_ref[here, lanes] = (scanned + lane_skip * g_here).astype(BF16)
            xd[here, lanes] = x_here * scanned
            gy[here, lanes] = g_here * yscan[here, lanes]
            gx[here, lanes] = g_here * x_here

    backward_pair(0)
    backward_pair(1)
    stage("b", 2)
    backward_pair(2)
    backward_pair(3)
    ring_stage(3, 1)
    backward_pair(4)

    head_of = lax.broadcasted_iota(jnp.int32, (16, WIDTH), 1) // PW
    pick = jnp.where(head_of == lax.broadcasted_iota(jnp.int32, (16, WIDTH), 0), 1.0, 0.0)
    entry_sum = dot_nt(pick, xd[...], HIGHEST)
    exit_sum = dot_nt(pick, gy[...], HIGHEST)
    skip_sum = dot_nt(pick, gx[...], HIGHEST)
    rate_grad = jnp.dot(
        entry_sum - exit_sum,
        jnp.where(first >= second, 1.0, 0.0),
        precision=HIGHEST,
        preferred_element_type=F32,
    )
    dt_now, decay_now = rows[1], rows[3]
    raw_grad = (entry_sum / dt_now + rate_grad * decay_now) * rows[2]
    dtg_ref[...] = raw_grad[0:HEADS, :]
    alog_part = jnp.sum(rate_grad * dt_now * decay_now, axis=1, keepdims=True)
    skip_part = jnp.sum(skip_sum, axis=1, keepdims=True)
    bias_part = jnp.sum(raw_grad, axis=1, keepdims=True)
    lane16 = lax.broadcasted_iota(jnp.int32, (16, HALF), 1)
    hbuf[i] = jnp.where(
        lane16 == 0, alog_part, jnp.where(lane16 == 1, skip_part, jnp.where(lane16 == 2, bias_part, 0.0))
    )
    for r in range(1, NDP):
        copy = heads_swap(r, False)
        copy.start()
        pending.append(copy)
    near_send(1, 1, 2)

    low_high, low_low = split(dgt[...])
    gg_ref[:, :NSTATE] = (dot(low_high, bc_buf[:, NSTATE:]) + dot(low_low, bc_buf[:, NSTATE:])).astype(BF16)
    up_high, up_low = split(jnp.transpose(dgt[...]))
    gg_ref[:, NSTATE:] = (dot(up_high, bc_buf[:, :NSTATE]) + dot(up_low, bc_buf[:, :NSTATE])).astype(BF16)

    def second_matmul(dvs, low, high):
        for p in range(2):
            slots = [slot_of(p, du, dv) for dv in dvs for du in range(4)]
            here = slice(p * T, (p + 1) * T)
            left_side = jnp.concatenate([b_buf[s, low * 16 : high * 16, here] for s in slots], axis=0)
            right_side = jnp.concatenate(
                [
                    outs[low:high, pl.ds(pl.multiple_of(s * 16, 16), 16), :].reshape((high - low) * 16, WIDTH)
                    for s in slots
                ],
                axis=0,
            )
            wg_ref[here, :] += dot_tn(left_side, right_side)

    def chip_matmul():
        for p in range(2):
            here = slice(p * T, (p + 1) * T)
            mine = a_buf[:, :, pl.ds(pl.multiple_of(i * DROWS + p * T, T), T)].reshape(T, T)
            left_side = jnp.concatenate([mine, near[0, :, :, here].reshape(T, T)], axis=0)
            wg_ref[here, :] = dot_tn(left_side, outs[FAR : FAR + 2, :, :].reshape(2 * T, WIDTH))

    def near_matmul(p):
        here = slice(p * T, (p + 1) * T)
        left_side = near[1:3, :, :, here].reshape(2 * T, T)
        wg_ref[here, :] += dot_tn(left_side, outs[FAR + 2 :, :, :].reshape(2 * T, WIDTH))

    near_wait((0, 1), 0)
    cross_waits((0, 1))
    chip_matmul()
    stage("b", 3)
    cross_waits((2, 3))
    second_matmul((0,), 0, MOST)
    stage("b", 4)
    ring_stage(4, 0)
    ring_stage(4, 1)
    near_wait((0,), 1, 2)
    near_matmul(0)
    second_matmul((1,), 0, MOST)
    second_matmul((-1,), 0, MOST)
    cross_waits((4,))
    second_matmul((0, 1, -1), MOST, FAR)
    near_wait((1,), 1, 2)
    near_matmul(1)
    for r in range(1, NDP):
        heads_swap(r, True).wait_recv()
    tot = hbuf[0]
    for r in range(1, NDP):
        tot = tot + hbuf[r]
    eye = jnp.where(
        lax.broadcasted_iota(jnp.int32, (8, HALF), 0) == lax.broadcasted_iota(jnp.int32, (8, HALF), 1), 1.0, 0.0
    )
    hg_ref[...] = dot_nt(eye, tot, HIGHEST)[0:3, 0:HEADS]
    last = 20
    for copy in pending[:-last]:
        copy.wait_send()
    stage("b", 5)
    second_matmul((2,), 0, FAR)
    for copy in pending[-last:]:
        copy.wait_send()


def publish(*refs):
    sems = refs[10]
    copies = [pltpu.make_async_copy(refs[n], refs[5 + n], sems.at[n]) for n in range(5)]
    for copy in copies:
        copy.start()
    for copy in copies:
        copy.wait()


def body(upstream, out_weight, inner, groups_bc, dt_raw, a_log, skip, dt_bias, head_counts):
    vmem = pl.BlockSpec(memory_space=pltpu.VMEM)
    hbm = pl.BlockSpec(memory_space=pl.ANY)
    dma = lambda n: pltpu.SemaphoreType.DMA((n,))
    shapes = (
        ((T, WIDTH), BF16),
        ((T, 2 * NSTATE), BF16),
        ((HEADS, T), F32),
        ((DROWS, WIDTH), F32),
        ((3, HEADS), F32),
    )
    results = pl.pallas_call(
        kernel,
        out_shape=tuple(pltpu.VMEM(*one) for one in shapes),
        in_specs=[hbm] * 9,
        out_specs=(vmem,) * 5,
        scratch_shapes=[
            pltpu.SMEM((HEADS,), F32),
            pltpu.SMEM((HEADS,), F32),
            pltpu.SMEM((HEADS,), F32),
            pltpu.SMEM((NT,), jnp.int32),
            pltpu.VMEM((HEADS, T), F32),
            pltpu.VMEM((NT, 16, D), BF16),
            pltpu.VMEM((NT, KB, DROWS), BF16),
            pltpu.VMEM((3, NT, 16, DROWS), BF16),
            pltpu.VMEM((NDP, T, WIDTH), BF16),
            pltpu.VMEM((D, WIDTH), BF16),
            pltpu.VMEM((T, WIDTH), BF16),
            pltpu.VMEM((T, 2 * NSTATE), BF16),
            pltpu.VMEM((4, 16, T), F32),
            pltpu.VMEM((T, HALF), F32),
            pltpu.VMEM((HALF, T), F32),
            pltpu.VMEM((T, T), F32),
            pltpu.VMEM((T, T), F32),
            pltpu.VMEM((T, WIDTH), F32),
            pltpu.VMEM((T, WIDTH), F32),
            pltpu.VMEM((T, T), F32),
            pltpu.VMEM((T, WIDTH), F32),
            pltpu.VMEM((T, WIDTH), F32),
            pltpu.VMEM((T, WIDTH), F32),
            pltpu.VMEM((NDP, 16, HALF), F32),
            dma(2 * NK), dma(2 * NK), dma(2 * NK), dma(2 * NK),
            dma(FAR), dma(FAR), dma(6), dma(6), dma(16), dma(16), dma(20), dma(20), dma(NDP), dma(NDP), dma(9),
        ],
        compiler_params=pltpu.CompilerParams(
            collective_id=0, has_side_effects=True, vmem_limit_bytes=56 * 1024 * 1024
        ),
    )(a_log, skip, dt_bias, head_counts, dt_raw, upstream, out_weight, inner, groups_bc)
    return pl.pallas_call(
        publish,
        out_shape=tuple(jax.ShapeDtypeStruct(*one) for one in shapes),
        in_specs=[vmem] * 5,
        out_specs=(hbm,) * 5,
        scratch_shapes=[dma(5)],
    )(*[pltpu.with_memory_space_constraint(one, pltpu.VMEM) for one in results])


def solution(mesh):
    return jax.shard_map(
        body,
        mesh=mesh,
        in_specs=(
            P(("dp", "tensor"), None),
            P(None, "tensor"),
            P("dp", "tensor"),
            P("dp", "tensor"),
            P("tensor", "dp"),
            P("tensor"),
            P("tensor"),
            P("tensor"),
            P(),
        ),
        out_specs=(
            P("dp", "tensor"),
            P("dp", "tensor"),
            P("tensor", "dp"),
            P("dp", "tensor"),
            P(None, "tensor"),
        ),
        check_vma=False,
    )
```
